512 devices in a mesh: dp: 32 (over x, z), tensor: 16 (over y, core).
Axes of the slice: x: 4, y: 8, z: 8, core: 2. Of those that a mesh axis runs over, the one named last changes fastest.
Arguments:
- policy_logits: bfloat16 [4096, 77824], P('dp', 'tensor'), may hold values from -50 to 250
- reference_logits: bfloat16 [4096, 77824], P('dp', 'tensor'), may hold values from -50 to 250
- targets: int32 [4096], P('dp'), may hold values from 0 to 77823
- loss_mask: int32 [4096], P('dp'), may hold values 0 or 1
- partner: int32 [256], P('dp'), may hold values from 0 to 255, as said below
- chosen: int32 [256], P('dp'), may hold values from 0 to 1, as said below
Outputs:
- logit_grad: float32 [4096, 77824], P('dp', 'tensor')
- pair_loss: float32 [256], P('dp')
The draws below stay inside these ranges and needn't reach their ends.
Inputs may be any that keep to these rules, and one draw needn't show every extreme that they name: partner[partner[s]] = s and partner[s] != s for every sequence s. Exactly one sequence of each pair has chosen = 1.
All inputs are finite; a program needn't handle non-finite values. No bound on the sum of `loss_mask` on one device may be relied on, other than what follows from the above.
Results may differ from the reference program's by a relative error of at most 0.0003.
Values may be sent and summed in bfloat16 or wider, within the bound.
A program may use at most 64 MiB of HBM per device.

```python
import math
import jax
import jax.numpy as jnp
from jax import lax

LEN = 16
ROWS = 4096
SEQS = 256
V = 77824


def shared_logits(key, rise_gain):
    key_list = jax.random.split(key, 2)
    column_scale = jnp.exp(jax.random.uniform(key_list[0], (V,), jnp.float32, math.log(0.4), math.log(4.0)))
    gauss_noise = jnp.clip(jax.random.normal(key_list[1], (ROWS, V), jnp.float32), -6.0, 6.0)
    noise_sum = gauss_noise
    columns = jnp.arange(V, dtype=jnp.int32)
    rise_curve = rise_gain * jnp.log1p(2.0 * columns.astype(jnp.float32) / V)
    return 1.8 * column_scale[None, :] * noise_sum + rise_curve[None, :]


def pairing(key):
    shuffled = jax.random.permutation(key, SEQS).astype(jnp.int32)
    first_half = shuffled[0::2]
    second_half = shuffled[1::2]
    flipped = jax.random.randint(jax.random.fold_in(key, 17), (SEQS // 2,), 0, 2).astype(jnp.int32)
    partner = jnp.zeros((SEQS,), jnp.int32).at[first_half].set(second_half).at[second_half].set(first_half)
    chosen = jnp.zeros((SEQS,), jnp.int32).at[first_half].set(flipped).at[second_half].set(1 - flipped)
    return (partner, chosen)


def draw_policy_logits(key, part):
    base_logits = shared_logits(key, 1.2)
    key = jax.random.fold_in(key, 3)
    own_noise = 0.5 * jnp.clip(jax.random.normal(key, (ROWS, V), jnp.float32), -6.0, 6.0)
    return (base_logits + own_noise).astype(jnp.bfloat16)


def draw_reference_logits(key, part):
    base_logits = shared_logits(key, 1.2)
    key = jax.random.fold_in(key, 4)
    own_noise = 0.3 * jnp.clip(jax.random.normal(key, (ROWS, V), jnp.float32), -6.0, 6.0)
    return (base_logits + own_noise).astype(jnp.bfloat16)


def draw_partner(key, part):
    result = pairing(key)[0]
    return result


def draw_chosen(key, part):
    result = pairing(key)[1]
    return result


def set_ends(values, own_key, smallest, largest):
    dims = values.shape
    place = [jax.random.randint(jax.random.fold_in(own_key, axis), (), 0, dims[axis]) for axis in range(len(dims))]
    values = values.at[tuple(place)].set(smallest)
    longest = dims.index(max(dims))
    place[longest] = (place[longest] + 1) % dims[longest]
    return values.at[tuple(place)].set(largest)


def setup_inputs(seed: int = 0) -> dict:
    keys = jax.random.split(jax.random.key(seed), 7)
    return {
        "policy_logits": draw_policy_logits(jax.random.fold_in(keys[6], 71), 0),
        "reference_logits": draw_reference_logits(jax.random.fold_in(keys[6], 71), 0),
        "targets": set_ends(jax.random.randint(keys[2], (ROWS,), 0, V), jax.random.fold_in(keys[2], 1), 0, V - 1).astype(jnp.int32),
        "loss_mask": set_ends((jax.random.randint(keys[3], (ROWS,), 0, 4) < 3).astype(jnp.int32), jax.random.fold_in(keys[3], 1), 0, 1),
        "partner": draw_partner(jax.random.fold_in(keys[6], 71), 0),
        "chosen": draw_chosen(jax.random.fold_in(keys[6], 71), 0),
    }


beta_scale = 0.5
kl_scale = 0.25


def row_numbers(seq_items):
    policy_part, refer_part, target_part = seq_items
    policy_vals = policy_part.astype(jnp.float32)
    refer_vals = refer_part.astype(jnp.float32)
    peak_policy = jnp.max(policy_vals, axis=-1, keepdims=True)
    total_policy = jnp.sum(jnp.exp(policy_vals - peak_policy), axis=-1)
    peak_refer = jnp.max(refer_vals, axis=-1, keepdims=True)
    expo_refer = jnp.exp(refer_vals - peak_refer)
    total_refer = jnp.sum(expo_refer, axis=-1)
    cross_sum = jnp.sum(expo_refer * (refer_vals - policy_vals), axis=-1)
    norm_policy = peak_policy[:, 0] + jnp.log(total_policy)
    norm_refer = peak_refer[:, 0] + jnp.log(total_refer)
    pick_policy = jnp.take_along_axis(policy_vals, target_part[:, None].astype(jnp.int32), axis=-1)[:, 0]
    pick_refer = jnp.take_along_axis(refer_vals, target_part[:, None].astype(jnp.int32), axis=-1)[:, 0]
    kl_row = cross_sum / total_refer - norm_refer + norm_policy
    ratio_row = (pick_policy - norm_policy) - (pick_refer - norm_refer)
    return ratio_row, kl_row, norm_policy, norm_refer


def reference(policy_logits, reference_logits, targets, loss_mask, partner, chosen):
    policy_seq = policy_logits.reshape(SEQS, LEN, V)
    refer_seq = reference_logits.reshape(SEQS, LEN, V)
    target_seq = targets.reshape(SEQS, LEN)
    mask_seq = loss_mask.reshape(SEQS, LEN).astype(jnp.float32)
    ratio_row, kl_row, norm_policy, norm_refer = lax.map(row_numbers, (policy_seq, refer_seq, target_seq))
    seq_ratio = jnp.sum(mask_seq * ratio_row, axis=1)
    seq_kl = jnp.sum(mask_seq * kl_row, axis=1)
    chosen_f = chosen.astype(jnp.float32)
    sign_value = 2.0 * chosen_f - 1.0
    margin = sign_value * (beta_scale * (seq_ratio - seq_ratio[partner]) + kl_scale * (seq_kl - seq_kl[partner]))
    pair_loss = jax.nn.softplus(-margin)
    slope_value = -jax.nn.sigmoid(-margin)
    coef_ratio = beta_scale * sign_value * slope_value
    coef_kl = -kl_scale * (1.0 - chosen_f) * slope_value
    columns = jnp.arange(V, dtype=jnp.int32)

    def grad_rows(seq_items):
        policy_part, refer_part, target_part, mask_part, lse_policy, lse_refer, c_ratio, c_kl = seq_items
        prob_policy = jnp.exp(policy_part.astype(jnp.float32) - lse_policy[:, None])
        prob_refer = jnp.exp(refer_part.astype(jnp.float32) - lse_refer[:, None])
        onehot = (columns[None, :] == target_part[:, None]).astype(jnp.float32)
        return mask_part[:, None] * (c_ratio * (onehot - prob_policy) + c_kl * (prob_policy - prob_refer))

    logit_grad = lax.map(grad_rows, (policy_seq, refer_seq, target_seq, mask_seq, norm_policy, norm_refer, coef_ratio, coef_kl))
    return logit_grad.reshape(ROWS, V), pair_loss
```

```python
import functools
import jax
import jax.numpy as jnp
from jax import lax
from jax.experimental import pallas as pl
from jax.experimental.pallas import tpu as pltpu
from jax.sharding import PartitionSpec as P

beta_scale = 0.5
kl_scale = 0.25
MESH = pl.DeviceIdType.MESH
LANES = 128
CHUNK = 16
TINY = -3.0e38


def stats_kernel(
    n_dp,
    n_tensor,
    p_hbm,
    r_hbm,
    targets_hbm,
    mask_hbm,
    partner_hbm,
    chosen_hbm,
    grad_ref,
    slope_ref,
    loss_ref,
    p_buf,
    r_buf,
    ep_buf,
    er_buf,
    rows_int,
    ids,
    lane_stats,
    column_set,
    own_rows,
    all_rows,
    own_seqs,
    all_seqs,
    chunk_sems,
    small_sems,
    row_send,
    row_recv,
    seq_send,
    seq_recv,
):
    rows, width = p_buf.shape
    tiles = width // LANES
    chunks = rows // CHUNK
    seqs = partner_hbm.shape[0]
    length = rows // seqs
    my_dp = lax.axis_index("dp")
    my_tensor = lax.axis_index("tensor")

    small = [
        pltpu.make_async_copy(targets_hbm, rows_int.at[0], small_sems.at[0]),
        pltpu.make_async_copy(mask_hbm, rows_int.at[1], small_sems.at[1]),
        pltpu.make_async_copy(partner_hbm, ids.at[0], small_sems.at[2]),
        pltpu.make_async_copy(chosen_hbm, ids.at[1], small_sems.at[3]),
    ]
    for copy in small:
        copy.start()

    def chunk_copies(c):
        here = pl.ds(pl.multiple_of(c * CHUNK, CHUNK), CHUNK)
        return (
            pltpu.make_async_copy(p_hbm.at[here], p_buf.at[here], chunk_sems.at[0, c]),
            pltpu.make_async_copy(r_hbm.at[here], r_buf.at[here], chunk_sems.at[1, c]),
        )

    for c in range(chunks):
        for copy in chunk_copies(c):
            copy.start()

    barrier = pltpu.get_barrier_semaphore()
    for k in range(1, n_tensor):
        pl.semaphore_signal(
            barrier,
            inc=1,
            device_id={"tensor": lax.rem(my_tensor + k, n_tensor)},
            device_id_type=MESH,
        )
    for k in range(1, n_dp):
        pl.semaphore_signal(
            barrier, inc=1, device_id={"dp": lax.rem(my_dp + k, n_dp)}, device_id_type=MESH
        )

    for copy in small:
        copy.wait()
    targets_row = rows_int[0:1, :] - my_tensor * width
    mask_row = rows_int[1:2, :].astype(jnp.float32)
    sub_r = lax.broadcasted_iota(jnp.int32, (LANES, LANES), 0)
    lane_r = lax.broadcasted_iota(jnp.int32, (LANES, LANES), 1)
    stacked = jnp.where(
        sub_r == 0, targets_row.astype(jnp.float32), jnp.where(sub_r == 1, mask_row, 0.0)
    )
    columns = stacked.T
    column_set[0] = (
        jnp.broadcast_to(columns[:, 0:1], (LANES, LANES)).astype(jnp.int32) - lane_r
    )
    mask_col = jnp.broadcast_to(columns[:, 1:2], (LANES, LANES))

    def one_chunk(c, carry):
        for copy in chunk_copies(c):
            copy.wait()
        here = pl.ds(pl.multiple_of(c * CHUNK, CHUNK), CHUNK)
        top_p = p_buf[here, pl.ds(0, LANES)]
        top_r = r_buf[here, pl.ds(0, LANES)]
        for t in range(1, tiles):
            top_p = jnp.maximum(top_p, p_buf[here, pl.ds(t * LANES, LANES)])
            top_r = jnp.maximum(top_r, r_buf[here, pl.ds(t * LANES, LANES)])
        top_p = top_p.astype(jnp.float32)
        top_r = top_r.astype(jnp.float32)
        hits = column_set[0, here, :]
        sum_p = jnp.zeros((CHUNK, LANES), jnp.float32)
        sum_r = sum_p
        cross = sum_p
        pick = sum_p
        for t in range(tiles):
            cols = pl.ds(t * LANES, LANES)
            p = p_buf[here, cols].astype(jnp.float32)
            r = r_buf[here, cols].astype(jnp.float32)
            e_p = jnp.exp(p - top_p)
            e_r = jnp.exp(r - top_r)
            gap = r - p
            ep_buf[here, cols] = e_p
            er_buf[here, cols] = e_r
            sum_p += e_p
            sum_r += e_r
            cross += e_r * gap
            pick += jnp.where(hits == t * LANES, gap, 0.0)
        lane_stats[0, here, :] = top_p
        lane_stats[1, here, :] = top_r
        lane_stats[2, here, :] = sum_p
        lane_stats[3, here, :] = sum_r
        lane_stats[4, here, :] = cross
        lane_stats[5, here, :] = pick
        return carry

    lax.fori_loop(0, chunks, one_chunk, 0)

    top_p = lane_stats[0]
    top_r = lane_stats[1]
    peak_p = jnp.max(top_p, axis=1, keepdims=True)
    peak_r = jnp.max(top_r, axis=1, keepdims=True)
    scale_p = jnp.exp(top_p - peak_p)
    scale_r = jnp.exp(top_r - peak_r)
    total_p = jnp.sum(lane_stats[2] * scale_p, axis=1, keepdims=True)
    total_r = jnp.sum(lane_stats[3] * scale_r, axis=1, keepdims=True)
    cross = jnp.sum(lane_stats[4] * scale_r, axis=1, keepdims=True)
    pick = jnp.sum(lane_stats[5], axis=1, keepdims=True)
    part_p = peak_p + jnp.log(total_p)
    part_r = peak_r + jnp.log(total_r)
    packed = jnp.where(
        lane_r == 0,
        part_p,
        jnp.where(
            lane_r == 1,
            part_r,
            jnp.where(lane_r == 2, cross / total_r, jnp.where(lane_r == 3, pick, 0.0)),
        ),
    )
    own = packed.T[0:8, :]
    own_rows[...] = own
    all_rows[my_tensor] = own

    pl.semaphore_wait(barrier, n_tensor + n_dp - 2)
    for k in range(1, n_tensor):
        pltpu.make_async_remote_copy(
            src_ref=own_rows,
            dst_ref=all_rows.at[my_tensor],
            send_sem=row_send,
            recv_sem=row_recv,
            device_id={"tensor": lax.rem(my_tensor + k, n_tensor)},
            device_id_type=MESH,
        ).start()

    sub_s = lax.broadcasted_iota(jnp.int32, (seqs, LANES), 0)
    lane_s = lax.broadcasted_iota(jnp.int32, (seqs, LANES), 1)
    partner_col = jnp.zeros((seqs, LANES), jnp.int32)
    chosen_col = jnp.zeros((seqs, LANES), jnp.float32)
    for j in range(seqs):
        partner_col = jnp.where(sub_s == j, ids[0, j], partner_col)
        chosen_col = jnp.where(sub_s == j, ids[1, j].astype(jnp.float32), chosen_col)
    sign_col = 2.0 * chosen_col - 1.0
    block_s = lane_s // length == sub_s

    others = all_rows.at[pl.ds(0, n_tensor - 1)]
    pltpu.make_async_copy(others, others, row_recv).wait()
    parts = [all_rows[k] for k in range(n_tensor)]
    peak = functools.reduce(jnp.maximum, parts)
    weights = [jnp.exp(part - peak) for part in parts]
    total = functools.reduce(jnp.add, weights)
    norm = peak + jnp.log(total)
    cross_row = functools.reduce(
        jnp.add, [w[1:2, :] * part[2:3, :] for w, part in zip(weights, parts)]
    )
    pick_row = functools.reduce(jnp.add, parts)[3:4, :]
    norm_p = norm[0:1, :]
    norm_r = norm[1:2, :]
    kl_row = cross_row / total[1:2, :] - norm_r + norm_p
    ratio_row = norm_r - norm_p - pick_row
    value_row = mask_row * (beta_scale * ratio_row + kl_scale * kl_row)
    own_col = jnp.sum(jnp.where(block_s, value_row, 0.0), axis=1, keepdims=True)
    own = jnp.sum(jnp.where(block_s, own_col, 0.0), axis=0, keepdims=True)
    own_seqs[...] = own
    all_seqs[pl.ds(my_dp, 1), :] = own

    for k in range(1, n_dp):
        pltpu.make_async_remote_copy(
            src_ref=own_seqs,
            dst_ref=all_seqs.at[pl.ds(my_dp, 1)],
            send_sem=seq_send,
            recv_sem=seq_recv,
            device_id={"dp": lax.rem(my_dp + k, n_dp)},
            device_id_type=MESH,
        ).start()

    stacked = jnp.where(sub_r == 0, norm_p, jnp.where(sub_r == 1, norm_r, 0.0))
    columns = stacked.T
    chosen_rows = jnp.concatenate(
        [jnp.broadcast_to(chosen_col[j : j + 1, :], (length, LANES)) for j in range(seqs)], axis=0
    )
    coef_hit = mask_col * (beta_scale * (2.0 * chosen_rows - 1.0))
    coef_kl = mask_col * (-kl_scale * (1.0 - chosen_rows))
    column_set[1] = coef_hit.astype(jnp.int32)
    lane_stats[2] = (coef_kl - coef_hit) * jnp.exp(lane_stats[0] - columns[:, 0:1])
    lane_stats[3] = coef_kl * jnp.exp(lane_stats[1] - columns[:, 1:2])
    lane_stats[4] = coef_hit

    def grad_chunk(c, carry):
        here = pl.ds(pl.multiple_of(c * CHUNK, CHUNK), CHUNK)
        hits = column_set[0, here, :]
        scale_p = lane_stats[2, here, :]
        scale_r = lane_stats[3, here, :]
        scale_hit = lane_stats[4, here, :]
        for t in range(tiles):
            cols = pl.ds(t * LANES, LANES)
            grad_ref[here, cols] = (
                ep_buf[here, cols] * scale_p
                - er_buf[here, cols] * scale_r
                + jnp.where(hits == t * LANES, scale_hit, 0.0)
            )
        return carry

    lax.fori_loop(0, chunks, grad_chunk, 0)

    others = all_seqs.at[pl.ds(0, n_dp - 1)]
    pltpu.make_async_copy(others, others, seq_recv).wait()
    table = all_seqs[...]
    place = length * seqs * lax.broadcasted_iota(jnp.int32, (n_dp, LANES), 0)
    place = place + lax.broadcasted_iota(jnp.int32, (n_dp, LANES), 1)
    found = [
        jnp.sum(jnp.where(place == ids[0, j] * length, table, 0.0), axis=0, keepdims=True)
        for j in range(seqs)
    ]
    partner_value = jnp.sum(jnp.concatenate(found, axis=0), axis=1, keepdims=True)
    margin = sign_col * (own_col - partner_value)
    slope_ref[...] = -jax.nn.sigmoid(-margin)
    loss_ref[...] = jnp.maximum(-margin, 0.0) + jnp.log1p(jnp.exp(-jnp.abs(margin)))

    sent = all_rows.at[pl.ds(0, n_tensor - 1)]
    pltpu.make_async_copy(sent, sent, row_send).wait()
    sent = all_seqs.at[pl.ds(0, n_dp - 1)]
    pltpu.make_async_copy(sent, sent, seq_send).wait()


def scale_kernel(grad_ref, slope_ref, out_hbm, out_buf, sems):
    rows, width = out_buf.shape
    seqs = slope_ref.shape[0]
    length = rows // seqs
    copies = []
    for j in range(seqs):
        here = pl.ds(j * length, length)
        out_buf[here, :] = grad_ref[here, :] * slope_ref[j : j + 1, 0:1]
        copy = pltpu.make_async_copy(out_buf.at[here], out_hbm.at[here], sems.at[j])
        copy.start()
        copies.append(copy)
    for copy in copies:
        copy.wait()


def shards(n_dp, n_tensor, policy_logits, reference_logits, targets, loss_mask, partner, chosen):
    rows, width = policy_logits.shape
    seqs = partner.shape[0]
    hbm = pl.BlockSpec(memory_space=pltpu.HBM)
    vmem = pl.BlockSpec(memory_space=pltpu.VMEM)
    grad, slope, loss = pl.pallas_call(
        functools.partial(stats_kernel, n_dp, n_tensor),
        out_shape=(
            pltpu.VMEM((rows, width), jnp.float32),
            pltpu.VMEM((seqs, LANES), jnp.float32),
            jax.ShapeDtypeStruct((seqs, LANES), jnp.float32),
        ),
        in_specs=[hbm] * 6,
        out_specs=(vmem, vmem, vmem),
        scratch_shapes=[
            pltpu.VMEM((rows, width), jnp.bfloat16),
            pltpu.VMEM((rows, width), jnp.bfloat16),
            pltpu.VMEM((rows, width), jnp.float32),
            pltpu.VMEM((rows, width), jnp.float32),
            pltpu.VMEM((2, rows), jnp.int32),
            pltpu.SMEM((2, seqs), jnp.int32),
            pltpu.VMEM((6, rows, LANES), jnp.float32),
            pltpu.VMEM((2, rows, LANES), jnp.int32),
            pltpu.VMEM((8, LANES), jnp.float32),
            pltpu.VMEM((n_tensor, 8, LANES), jnp.float32),
            pltpu.VMEM((1, LANES), jnp.float32),
            pltpu.VMEM((n_dp, LANES), jnp.float32),
            pltpu.SemaphoreType.DMA((2, rows // CHUNK)),
            pltpu.SemaphoreType.DMA((4,)),
            pltpu.SemaphoreType.DMA,
            pltpu.SemaphoreType.DMA,
            pltpu.SemaphoreType.DMA,
            pltpu.SemaphoreType.DMA,
        ],
        compiler_params=pltpu.CompilerParams(
            collective_id=0, has_side_effects=True, vmem_limit_bytes=32 * 1024 * 1024
        ),
        name="row_stats",
    )(policy_logits, reference_logits, targets, loss_mask, partner, chosen)
    logit_grad = pl.pallas_call(
        scale_kernel,
        out_shape=jax.ShapeDtypeStruct((rows, width), jnp.float32),
        in_specs=[vmem, vmem],
        out_specs=hbm,
        scratch_shapes=[
            pltpu.VMEM((rows, width), jnp.float32),
            pltpu.SemaphoreType.DMA((seqs,)),
        ],
        compiler_params=pltpu.CompilerParams(vmem_limit_bytes=32 * 1024 * 1024),
        name="scale_grad",
    )(grad, slope)
    return logit_grad, loss[:, 0]


def solution(mesh):
    return jax.shard_map(
        functools.partial(shards, mesh.shape["dp"], mesh.shape["tensor"]),
        mesh=mesh,
        in_specs=(P("dp", "tensor"), P("dp", "tensor"), P("dp"), P("dp"), P("dp"), P("dp")),
        out_specs=(P("dp", "tensor"), P("dp")),
        check_vma=False,
    )
```

```python
import functools
import jax
import jax.numpy as jnp
from jax import lax
from jax.experimental import pallas as pl
from jax.experimental.pallas import tpu as pltpu
from jax.sharding import PartitionSpec as P

beta_scale = 0.5
kl_scale = 0.25
MESH = pl.DeviceIdType.MESH
LANES = 128
CHUNK = 16
PARTS = 4


def ring(size):
    return sorted(range(1, size), key=lambda k: -min(k, size - k))


def stats_kernel(
    n_dp,
    n_tensor,
    n_z,
    p_hbm,
    r_hbm,
    targets_hbm,
    mask_hbm,
    partner_hbm,
    chosen_hbm,
    grad_ref,
    margin_ref,
    p_buf,
    r_buf,
    rows_int,
    ids,
    lane_stats,
    hit_set,
    own_rows,
    all_rows,
    own_seqs,
    all_seqs,
    chunk_sems,
    small_sems,
    row_send,
    row_recv,
    seq_send,
    seq_recv,
    known_sem,
):
    rows, width = p_buf.shape
    tiles = width // LANES
    chunks = rows // CHUNK
    seqs = partner_hbm.shape[0]
    length = rows // seqs
    n_x = n_dp // n_z
    my_dp = lax.axis_index("dp")
    my_tensor = lax.axis_index("tensor")
    my_x = my_dp // n_z
    my_z = lax.rem(my_dp, n_z)

    def tensor_peer(k):
        return {"tensor": lax.rem(my_tensor + k, n_tensor)}

    def dp_peer(x, z):
        return {"dp": lax.rem(my_x + x, n_x) * n_z + lax.rem(my_z + z, n_z)}

    barrier = pltpu.get_barrier_semaphore()
    greeted = [tensor_peer(k) for k in ring(n_tensor)]
    greeted += [dp_peer(0, z) for z in ring(n_z)]
    greeted += [dp_peer(x, 0) for x in ring(n_x)]
    for peer in greeted:
        pl.semaphore_signal(barrier, inc=1, device_id=peer, device_id_type=MESH)

    small = [
        pltpu.make_async_copy(targets_hbm, rows_int.at[0], small_sems.at[0]),
        pltpu.make_async_copy(mask_hbm, rows_int.at[1], small_sems.at[1]),
        pltpu.make_async_copy(partner_hbm, ids.at[0], small_sems.at[2]),
        pltpu.make_async_copy(chosen_hbm, ids.at[1], small_sems.at[3]),
    ]
    for copy in small:
        copy.start()

    def chunk_copies(c):
        here = pl.ds(pl.multiple_of(c * CHUNK, CHUNK), CHUNK)
        return (
            pltpu.make_async_copy(p_hbm.at[here], p_buf.at[here], chunk_sems.at[0, c]),
            pltpu.make_async_copy(r_hbm.at[here], r_buf.at[here], chunk_sems.at[1, c]),
        )

    for c in range(chunks):
        for copy in chunk_copies(c):
            copy.start()

    for copy in small:
        copy.wait()
    targets_row = rows_int[0:1, :] - my_tensor * width
    mask_row = rows_int[1:2, :].astype(jnp.float32)
    sub_r = lax.broadcasted_iota(jnp.int32, (LANES, LANES), 0)
    lane_r = lax.broadcasted_iota(jnp.int32, (LANES, LANES), 1)
    stacked = jnp.where(
        sub_r == 0, targets_row.astype(jnp.float32), jnp.where(sub_r == 1, mask_row, 0.0)
    )
    columns = stacked.T
    hit_set[...] = jnp.broadcast_to(columns[:, 0:1], (LANES, LANES)).astype(jnp.int32) - lane_r
    mask_col = columns[:, 1:2]

    def one_chunk(c, carry):
        for copy in chunk_copies(c):
            copy.wait()
        here = pl.ds(pl.multiple_of(c * CHUNK, CHUNK), CHUNK)
        top_p = p_buf[here, pl.ds(0, LANES)]
        top_r = r_buf[here, pl.ds(0, LANES)]
        for t in range(1, tiles):
            top_p = jnp.maximum(top_p, p_buf[here, pl.ds(t * LANES, LANES)])
            top_r = jnp.maximum(top_r, r_buf[here, pl.ds(t * LANES, LANES)])
        top_p = top_p.astype(jnp.float32)
        top_r = top_r.astype(jnp.float32)
        hits = hit_set[here, :]
        sum_p = jnp.zeros((CHUNK, LANES), jnp.float32)
        sum_r = sum_p
        cross = sum_p
        pick = sum_p
        for t in range(tiles):
            cols = pl.ds(t * LANES, LANES)
            p = p_buf[here, cols].astype(jnp.float32)
            r = r_buf[here, cols].astype(jnp.float32)
            e_p = jnp.exp(p - top_p)
            e_r = jnp.exp(r - top_r)
            gap = r - p
            sum_p += e_p
            sum_r += e_r
            cross += e_r * gap
            pick += jnp.where(hits == t * LANES, gap, 0.0)
        lane_stats[0, here, :] = top_p
        lane_stats[1, here, :] = top_r
        lane_stats[2, here, :] = sum_p
        lane_stats[3, here, :] = sum_r
        lane_stats[4, here, :] = cross
        lane_stats[5, here, :] = pick
        return carry

    lax.fori_loop(0, chunks, one_chunk, 0)

    top_p = lane_stats[0]
    top_r = lane_stats[1]
    peak_p = jnp.max(top_p, axis=1, keepdims=True)
    peak_r = jnp.max(top_r, axis=1, keepdims=True)
    scale_r = jnp.exp(top_r - peak_r)
    total_p = jnp.sum(lane_stats[2] * jnp.exp(top_p - peak_p), axis=1, keepdims=True)
    total_r = jnp.sum(lane_stats[3] * scale_r, axis=1, keepdims=True)
    cross = jnp.sum(lane_stats[4] * scale_r, axis=1, keepdims=True)
    pick = jnp.sum(lane_stats[5], axis=1, keepdims=True)
    part_p = peak_p + jnp.log(total_p)
    part_r = peak_r + jnp.log(total_r)
    packed = jnp.where(
        lane_r == 0,
        part_p,
        jnp.where(
            lane_r == 1,
            part_r,
            jnp.where(lane_r == 2, cross / total_r, jnp.where(lane_r == 3, pick, 0.0)),
        ),
    )
    own = packed.T[0:PARTS, :]
    own_rows[...] = own
    all_rows[my_tensor] = own

    pl.semaphore_wait(barrier, len(greeted))
    for k in ring(n_tensor):
        pltpu.make_async_remote_copy(
            src_ref=own_rows,
            dst_ref=all_rows.at[my_tensor],
            send_sem=row_send,
            recv_sem=row_recv,
            device_id=tensor_peer(k),
            device_id_type=MESH,
        ).start()

    for x in ring(n_x):
        pl.semaphore_signal(known_sem, inc=1, device_id=dp_peer(x, 0), device_id_type=MESH)

    sub_s = lax.broadcasted_iota(jnp.int32, (seqs, LANES), 0)
    lane_s = lax.broadcasted_iota(jnp.int32, (seqs, LANES), 1)
    place_col = jnp.zeros((seqs, LANES), jnp.int32)
    chosen_col = jnp.zeros((seqs, LANES), jnp.float32)
    for j in range(seqs):
        place_col = jnp.where(sub_s == j, lax.rem(ids[0, j], seqs) * length, place_col)
        chosen_col = jnp.where(sub_s == j, ids[1, j].astype(jnp.float32), chosen_col)
    sign_col = 2.0 * chosen_col - 1.0
    block_s = lane_s // length == sub_s

    pl.semaphore_wait(known_sem, n_x - 1)
    others = all_rows.at[pl.ds(0, n_tensor - 1)]
    pltpu.make_async_copy(others, others, row_recv).wait()
    parts = [all_rows[k] for k in range(n_tensor)]
    peak = functools.reduce(jnp.maximum, parts)
    weights = [jnp.exp(part - peak) for part in parts]
    total = functools.reduce(jnp.add, weights)
    norm = peak + jnp.log(total)
    cross_row = functools.reduce(
        jnp.add, [w[1:2, :] * part[2:3, :] for w, part in zip(weights, parts)]
    )
    pick_row = functools.reduce(jnp.add, parts)[3:4, :]
    norm_p = norm[0:1, :]
    norm_r = norm[1:2, :]
    kl_row = cross_row / total[1:2, :] - norm_r + norm_p
    ratio_row = norm_r - norm_p - pick_row
    value_row = mask_row * (beta_scale * ratio_row + kl_scale * kl_row)
    own_col = jnp.sum(jnp.where(block_s, value_row, 0.0), axis=1, keepdims=True)
    own = jnp.sum(jnp.where(block_s, own_col, 0.0), axis=0, keepdims=True)
    own_seqs[...] = own
    all_seqs[pl.ds(my_dp, 1), :] = own

    far = sorted(
        [(x, z) for x in range(n_x) for z in range(n_z) if x or z],
        key=lambda s: -min(s[0], n_x - s[0]) - min(s[1], n_z - s[1]),
    )
    for x, z in far:
        pltpu.make_async_remote_copy(
            src_ref=own_seqs,
            dst_ref=all_seqs.at[pl.ds(my_dp, 1)],
            send_sem=seq_send,
            recv_sem=seq_recv,
            device_id=dp_peer(x, z),
            device_id_type=MESH,
        ).start()

    stacked = jnp.where(sub_r == 0, norm_p, jnp.where(sub_r == 1, norm_r, 0.0))
    columns = stacked.T
    chosen_rows = jnp.concatenate(
        [jnp.broadcast_to(chosen_col[j : j + 1, :], (length, LANES)) for j in range(seqs)], axis=0
    )
    coef_hit = mask_col * (beta_scale * (2.0 * chosen_rows - 1.0))
    coef_kl = mask_col * (-kl_scale * (1.0 - chosen_rows))
    lane_stats[0] = jnp.broadcast_to(columns[:, 0:1], (LANES, LANES))
    lane_stats[1] = jnp.broadcast_to(columns[:, 1:2], (LANES, LANES))
    lane_stats[2] = coef_kl - coef_hit
    lane_stats[3] = coef_kl
    lane_stats[4] = coef_hit

    def grad_chunk(c, carry):
        here = pl.ds(pl.multiple_of(c * CHUNK, CHUNK), CHUNK)
        hits = hit_set[here, :]
        base_p = lane_stats[0, here, :]
        base_r = lane_stats[1, here, :]
        scale_p = lane_stats[2, here, :]
        scale_r = lane_stats[3, here, :]
        scale_hit = lane_stats[4, here, :]
        for t in range(tiles):
            cols = pl.ds(t * LANES, LANES)
            p = p_buf[here, cols].astype(jnp.float32)
            r = r_buf[here, cols].astype(jnp.float32)
            grad_ref[here, cols] = (
                jnp.exp(p - base_p) * scale_p
                - jnp.exp(r - base_r) * scale_r
                + jnp.where(hits == t * LANES, scale_hit, 0.0)
            )
        return carry

    lax.fori_loop(0, chunks, grad_chunk, 0)

    pltpu.make_async_copy(others, others, row_send).wait()
    others = all_seqs.at[pl.ds(0, n_dp - 1)]
    pltpu.make_async_copy(others, others, seq_send).wait()
    pltpu.make_async_copy(others, others, seq_recv).wait()
    partner_rows = jnp.zeros((seqs, LANES), jnp.float32)
    for j in range(seqs):
        row = all_seqs[pl.ds(ids[0, j] // seqs, 1), :]
        partner_rows = jnp.where(sub_s == j, row, partner_rows)
    partner_value = jnp.sum(
        jnp.where(lane_s == place_col, partner_rows, 0.0), axis=1, keepdims=True
    )
    margin_ref[...] = sign_col * (own_col - partner_value)


def scale_kernel(grad_ref, margin_ref, out_hbm, loss_hbm, out_buf, loss_buf, sems):
    rows, width = out_buf.shape
    seqs = margin_ref.shape[0]
    length = rows // seqs
    margin = margin_ref[...]
    slope = -jax.nn.sigmoid(-margin)
    copies = []
    for j in range(seqs):
        here = pl.ds(j * length, length)
        out_buf[here, :] = grad_ref[here, :] * slope[j : j + 1, 0:1]
        copy = pltpu.make_async_copy(out_buf.at[here], out_hbm.at[here], sems.at[j])
        copy.start()
        copies.append(copy)
    loss = jnp.maximum(-margin, 0.0) + jnp.log1p(jnp.exp(-jnp.abs(margin)))
    sub = lax.broadcasted_iota(jnp.int32, (seqs, LANES), 0)
    lane = lax.broadcasted_iota(jnp.int32, (seqs, LANES), 1)
    loss_buf[...] = jnp.sum(jnp.where(sub == lane, loss, 0.0), axis=0)[:seqs]
    copy = pltpu.make_async_copy(loss_buf, loss_hbm, sems.at[seqs])
    copy.start()
    copies.append(copy)
    for copy in copies:
        copy.wait()


def shards(n_dp, n_tensor, n_z, *arrays):
    rows, width = arrays[0].shape
    seqs = arrays[4].shape[0]
    hbm = pl.BlockSpec(memory_space=pltpu.HBM)
    vmem = pl.BlockSpec(memory_space=pltpu.VMEM)
    arrays = [pltpu.with_memory_space_constraint(array, pltpu.HBM) for array in arrays]
    grad, margin = pl.pallas_call(
        functools.partial(stats_kernel, n_dp, n_tensor, n_z),
        out_shape=(
            pltpu.VMEM((rows, width), jnp.float32),
            pltpu.VMEM((seqs, LANES), jnp.float32),
        ),
        in_specs=[hbm] * 6,
        out_specs=(vmem, vmem),
        scratch_shapes=[
            pltpu.VMEM((rows, width), jnp.bfloat16),
            pltpu.VMEM((rows, width), jnp.bfloat16),
            pltpu.VMEM((2, rows), jnp.int32),
            pltpu.SMEM((2, seqs), jnp.int32),
            pltpu.VMEM((6, rows, LANES), jnp.float32),
            pltpu.VMEM((rows, LANES), jnp.int32),
            pltpu.VMEM((PARTS, LANES), jnp.float32),
            pltpu.VMEM((n_tensor, PARTS, LANES), jnp.float32),
            pltpu.VMEM((1, LANES), jnp.float32),
            pltpu.VMEM((n_dp, LANES), jnp.float32),
            pltpu.SemaphoreType.DMA((2, rows // CHUNK)),
            pltpu.SemaphoreType.DMA((4,)),
            pltpu.SemaphoreType.DMA,
            pltpu.SemaphoreType.DMA,
            pltpu.SemaphoreType.DMA,
            pltpu.SemaphoreType.DMA,
            pltpu.SemaphoreType.REGULAR,
        ],
        compiler_params=pltpu.CompilerParams(
            collective_id=0, has_side_effects=True, vmem_limit_bytes=32 * 1024 * 1024
        ),
        name="row_stats",
    )(*arrays)
    return pl.pallas_call(
        scale_kernel,
        out_shape=(
            jax.ShapeDtypeStruct((rows, width), jnp.float32),
            jax.ShapeDtypeStruct((seqs,), jnp.float32),
        ),
        in_specs=[vmem, vmem],
        out_specs=(hbm, hbm),
        scratch_shapes=[
            pltpu.VMEM((rows, width), jnp.float32),
            pltpu.VMEM((seqs,), jnp.float32),
            pltpu.SemaphoreType.DMA((seqs + 1,)),
        ],
        compiler_params=pltpu.CompilerParams(vmem_limit_bytes=32 * 1024 * 1024),
        name="scale_grad",
    )(grad, margin)


def solution(mesh):
    n_dp, n_tensor = mesh.shape["dp"], mesh.shape["tensor"]
    n_z = 8 if n_dp % 8 == 0 and n_dp > 8 else n_dp // 2
    return jax.shard_map(
        functools.partial(shards, n_dp, n_tensor, n_z),
        mesh=mesh,
        in_specs=(P("dp", "tensor"), P("dp", "tensor"), P("dp"), P("dp"), P("dp"), P("dp")),
        out_specs=(P("dp", "tensor"), P("dp")),
        check_vma=False,
    )
```

```python
import functools
import jax
import jax.numpy as jnp
from jax import lax
from jax.experimental import pallas as pl
from jax.experimental.pallas import tpu as pltpu
from jax.sharding import PartitionSpec as P

beta_scale = 0.5
kl_scale = 0.25
MESH = pl.DeviceIdType.MESH
LANES = 128
CHUNK = 16
GROUP = 32
WAYS = 4
PARTS = 4
CORES = 2


def ring(size):
    return sorted(range(1, size), key=lambda k: -min(k, size - k))


def stats_kernel(
    n_dp,
    n_tensor,
    n_z,
    p_hbm,
    r_hbm,
    targets_hbm,
    mask_hbm,
    partner_hbm,
    chosen_hbm,
    grad_ref,
    margin_ref,
    p_buf,
    r_buf,
    rows_int,
    ids,
    lane_stats,
    hit_set,
    own_rows,
    all_rows,
    own_seqs,
    all_seqs,
    group_sems,
    small_sems,
    row_send,
    row_recv,
    seq_send,
    seq_recv,
    known_sems,
):
    rows, width = p_buf.shape
    tiles = width // LANES
    chunks = rows // CHUNK
    seqs = partner_hbm.shape[0]
    length = rows // seqs
    n_x = n_dp // n_z
    my_dp = lax.axis_index("dp")
    my_tensor = lax.axis_index("tensor")
    my_x = my_dp // n_z
    my_z = lax.rem(my_dp, n_z)

    my_y = my_tensor // CORES
    my_core = lax.rem(my_tensor, CORES)
    n_y = n_tensor // CORES
    sibling = {"tensor": my_tensor + 1 - 2 * my_core}

    def y_peer(y, core):
        return {"tensor": lax.rem(my_y + y, n_y) * CORES + core}

    def tensor_peer(k):
        return {"tensor": lax.rem(my_tensor + k, n_tensor)}

    def dp_peer(x, z):
        place = lax.rem(my_x + x, n_x) * n_z + lax.rem(my_z + z, n_z)
        return {"dp": place, "tensor": my_y * CORES + 1}

    def signal(sem, peer):
        pl.semaphore_signal(sem, inc=1, device_id=peer, device_id_type=MESH)

    small = [
        pltpu.make_async_copy(targets_hbm, rows_int.at[0], small_sems.at[0]),
        pltpu.make_async_copy(mask_hbm, rows_int.at[1], small_sems.at[1]),
        pltpu.make_async_copy(partner_hbm, ids.at[0], small_sems.at[2]),
        pltpu.make_async_copy(chosen_hbm, ids.at[1], small_sems.at[3]),
    ]
    def group_copies(c):
        here = pl.ds(pl.multiple_of(c * GROUP, GROUP), GROUP)
        return (
            pltpu.make_async_copy(p_hbm.at[here], p_buf.at[here], group_sems.at[0, c]),
            pltpu.make_async_copy(r_hbm.at[here], r_buf.at[here], group_sems.at[1, c]),
        )

    for copy in small[:2]:
        copy.start()
    for copy in group_copies(0):
        copy.start()

    barrier = pltpu.get_barrier_semaphore()
    greeted = [(min(y, n_y - y), y_peer(y, 0)) for y in range(1, n_y)]
    greeted += [(min(z, n_z - z), dp_peer(0, z)) for z in range(1, n_z)]
    greeted += [(min(x, n_x - x), dp_peer(x, 0)) for x in range(1, n_x)]
    for _, peer in sorted(greeted, key=lambda g: -g[0]):
        signal(barrier, peer)
    signal(barrier, sibling)

    for c in range(1, rows // GROUP):
        for copy in group_copies(c):
            copy.start()
    for copy in small[2:]:
        copy.start()

    for copy in small[:2]:
        copy.wait()
    targets_row = rows_int[0:1, :] - my_tensor * width
    mask_row = rows_int[1:2, :].astype(jnp.float32)
    sub_r = lax.broadcasted_iota(jnp.int32, (LANES, LANES), 0)
    lane_r = lax.broadcasted_iota(jnp.int32, (LANES, LANES), 1)
    stacked = jnp.where(
        sub_r == 0, targets_row.astype(jnp.float32), jnp.where(sub_r == 1, mask_row, 0.0)
    )
    columns = stacked.T
    hit_set[...] = jnp.broadcast_to(columns[:, 0:1], (LANES, LANES)).astype(jnp.int32) - lane_r
    mask_col = columns[:, 1:2]

    diagonal = (
        lax.broadcasted_iota(jnp.int32, (8, LANES), 1)
        - lax.broadcasted_iota(jnp.int32, (8, LANES), 0)
    )

    def peak_of(buf, here):
        tops = [buf[here, pl.ds(t * LANES, LANES)] for t in range(WAYS)]
        for t in range(WAYS, tiles):
            tops[t % WAYS] = jnp.maximum(tops[t % WAYS], buf[here, pl.ds(t * LANES, LANES)])
        return functools.reduce(jnp.maximum, tops).astype(jnp.float32)

    def sums_of(start):
        here = pl.ds(pl.multiple_of(start, CHUNK), CHUNK)
        top_p = peak_of(p_buf, here)
        top_r = peak_of(r_buf, here)
        peak_p = jnp.max(top_p, axis=1, keepdims=True)
        peak_r = jnp.max(top_r, axis=1, keepdims=True)
        scale_p = jnp.exp(top_p - peak_p)
        scale_r = jnp.exp(top_r - peak_r)
        hits = hit_set[here, :]
        sum_p = jnp.zeros((CHUNK, LANES), jnp.float32)
        sum_r = sum_p
        cross = sum_p
        pick = sum_p
        for t in range(tiles):
            cols = pl.ds(t * LANES, LANES)
            p = p_buf[here, cols].astype(jnp.float32)
            r = r_buf[here, cols].astype(jnp.float32)
            e_p = jnp.exp(p - top_p)
            e_r = jnp.exp(r - top_r)
            gap = r - p
            sum_p += e_p
            sum_r += e_r
            cross += e_r * gap
            pick = jnp.where(hits == t * LANES, gap, pick)
        return sum_p * scale_p, sum_r * scale_r, cross * scale_r, pick, peak_p, peak_r

    def add_rows(acc, start, sums):
        total_p, total_r, cross, pick = [
            jnp.sum(part, axis=1, keepdims=True) for part in sums[:4]
        ]
        part_p = sums[4] + jnp.log(total_p)
        part_r = sums[5] + jnp.log(total_r)
        columns = (part_p, part_r, cross / total_r, pick)
        out = []
        for total, column in zip(acc, columns):
            for g in range(0, CHUNK, 8):
                total = total + jnp.where(diagonal == start + g, column[g : g + 8, :], 0.0)
            out.append(total)
        return tuple(out)

    def one_group(c, carry):
        acc, before = carry
        for copy in group_copies(c):
            copy.wait()
        for g in range(0, GROUP, CHUNK):
            start = c * GROUP + g
            sums = sums_of(start)
            acc = add_rows(acc, start - CHUNK, before)
            before = sums
        return acc, before

    ones = jnp.ones((CHUNK, LANES), jnp.float32)
    column = jnp.zeros((CHUNK, 1), jnp.float32)
    zero = jnp.zeros((8, LANES), jnp.float32)
    start = ((zero,) * PARTS, (ones, ones, ones, ones, column, column))
    acc, sums = lax.fori_loop(0, rows // GROUP, one_group, start)
    acc = add_rows(acc, rows - CHUNK, sums)

    for k in range(PARTS):
        own_rows[k : k + 1, :] = jnp.sum(acc[k], axis=0, keepdims=True)
    all_rows[my_tensor] = own_rows[...]

    @pl.when(my_core == 0)
    def _():
        pl.semaphore_wait(barrier, 2 * n_y - 1)
        signal(known_sems.at[0], sibling)

    @pl.when(my_core == 1)
    def _():
        pl.semaphore_wait(known_sems.at[0], 1)

    for k in ring(n_tensor):
        pltpu.make_async_remote_copy(
            src_ref=own_rows,
            dst_ref=all_rows.at[my_tensor],
            send_sem=row_send,
            recv_sem=row_recv,
            device_id=tensor_peer(k),
            device_id_type=MESH,
        ).start()

    @pl.when(my_core == 1)
    def _():
        pl.semaphore_wait(barrier, 2 * (n_z + n_x) - 3)
        for x in ring(n_x):
            signal(known_sems.at[1], dp_peer(x, 0))
        pl.semaphore_wait(known_sems.at[1], n_x - 1)
        signal(known_sems.at[2], sibling)

    @pl.when(my_core == 0)
    def _():
        pl.semaphore_wait(known_sems.at[2], 1)

    for copy in small[2:]:
        copy.wait()

    sub_s = lax.broadcasted_iota(jnp.int32, (seqs, LANES), 0)
    lane_s = lax.broadcasted_iota(jnp.int32, (seqs, LANES), 1)
    place_col = jnp.zeros((seqs, LANES), jnp.int32)
    chosen_col = jnp.zeros((seqs, LANES), jnp.float32)
    for j in range(seqs):
        place_col = jnp.where(sub_s == j, lax.rem(ids[0, j], seqs) * length, place_col)
        chosen_col = jnp.where(sub_s == j, ids[1, j].astype(jnp.float32), chosen_col)
    sign_col = 2.0 * chosen_col - 1.0
    block_s = lane_s // length == sub_s

    others = all_rows.at[pl.ds(0, n_tensor - 1)]
    pltpu.make_async_copy(others, others, row_recv).wait()
    parts = [all_rows[k] for k in range(n_tensor)]
    peak = functools.reduce(jnp.maximum, parts)
    weights = [jnp.exp(part - peak) for part in parts]
    total = functools.reduce(jnp.add, weights)
    norm = peak + jnp.log(total)
    cross_row = functools.reduce(
        jnp.add, [w[1:2, :] * part[2:3, :] for w, part in zip(weights, parts)]
    )
    pick_row = functools.reduce(jnp.add, parts)[3:4, :]
    norm_p = norm[0:1, :]
    norm_r = norm[1:2, :]
    kl_row = cross_row / total[1:2, :] - norm_r + norm_p
    ratio_row = norm_r - norm_p - pick_row
    value_row = mask_row * (beta_scale * ratio_row + kl_scale * kl_row)
    own_col = jnp.sum(jnp.where(block_s, value_row, 0.0), axis=1, keepdims=True)
    own = jnp.sum(jnp.where(block_s, own_col, 0.0), axis=0, keepdims=True)
    own_seqs[...] = own
    all_seqs[pl.ds(my_dp, 1), :] = own

    my_rank = my_z * n_x + my_x
    for k in range(n_dp - 1):
        rank = k + (k + n_dp - my_rank) // n_dp
        pltpu.make_async_remote_copy(
            src_ref=own_seqs,
            dst_ref=all_seqs.at[pl.ds(my_dp, 1)],
            send_sem=seq_send,
            recv_sem=seq_recv,
            device_id={"dp": lax.rem(rank, n_x) * n_z + rank // n_x},
            device_id_type=MESH,
        ).start()

    stacked = jnp.where(sub_r == 0, norm_p, jnp.where(sub_r == 1, norm_r, 0.0))
    columns = stacked.T
    chosen_rows = jnp.concatenate(
        [jnp.broadcast_to(chosen_col[j : j + 1, :], (length, LANES)) for j in range(seqs)], axis=0
    )
    coef_hit = mask_col * (beta_scale * (2.0 * chosen_rows - 1.0))
    coef_kl = mask_col * (-kl_scale * (1.0 - chosen_rows))
    lane_stats[0] = jnp.broadcast_to(columns[:, 0:1], (LANES, LANES))
    lane_stats[1] = jnp.broadcast_to(columns[:, 1:2], (LANES, LANES))
    lane_stats[2] = coef_kl - coef_hit
    lane_stats[3] = coef_kl
    lane_stats[4] = coef_hit

    def grad_chunk(c, carry):
        here = pl.ds(pl.multiple_of(c * CHUNK, CHUNK), CHUNK)
        hits = hit_set[here, :]
        base_p = lane_stats[0, here, :]
        base_r = lane_stats[1, here, :]
        scale_p = lane_stats[2, here, :]
        scale_r = lane_stats[3, here, :]
        scale_hit = lane_stats[4, here, :]
        for t in range(tiles):
            cols = pl.ds(t * LANES, LANES)
            p = p_buf[here, cols].astype(jnp.float32)
            r = r_buf[here, cols].astype(jnp.float32)
            grad_ref[here, cols] = (
                jnp.exp(p - base_p) * scale_p
                - jnp.exp(r - base_r) * scale_r
                + jnp.where(hits == t * LANES, scale_hit, 0.0)
            )
        return carry

    lax.fori_loop(0, chunks, grad_chunk, 0)

    pltpu.make_async_copy(others, others, row_send).wait()
    others = all_seqs.at[pl.ds(0, n_dp - 1)]
    pltpu.make_async_copy(others, others, seq_send).wait()
    pltpu.make_async_copy(others, others, seq_recv).wait()
    partner_rows = jnp.zeros((seqs, LANES), jnp.float32)
    for j in range(seqs):
        row = all_seqs[pl.ds(ids[0, j] // seqs, 1), :]
        partner_rows = jnp.where(sub_s == j, row, partner_rows)
    partner_value = jnp.sum(
        jnp.where(lane_s == place_col, partner_rows, 0.0), axis=1, keepdims=True
    )
    margin_ref[...] = sign_col * (own_col - partner_value)


def scale_kernel(grad_ref, margin_ref, out_hbm, loss_hbm, out_buf, loss_buf, sems):
    rows, width = out_buf.shape
    seqs = margin_ref.shape[0]
    length = rows // seqs
    margin = margin_ref[...]
    slope = -jax.nn.sigmoid(-margin)
    copies = []
    for j in range(seqs):
        here = pl.ds(j * length, length)
        out_buf[here, :] = grad_ref[here, :] * slope[j : j + 1, 0:1]
        copy = pltpu.make_async_copy(out_buf.at[here], out_hbm.at[here], sems.at[j])
        copy.start()
        copies.append(copy)
    loss = jnp.maximum(-margin, 0.0) + jnp.log1p(jnp.exp(-jnp.abs(margin)))
    sub = lax.broadcasted_iota(jnp.int32, (seqs, LANES), 0)
    lane = lax.broadcasted_iota(jnp.int32, (seqs, LANES), 1)
    loss_buf[...] = jnp.sum(jnp.where(sub == lane, loss, 0.0), axis=0)[:seqs]
    copy = pltpu.make_async_copy(loss_buf, loss_hbm, sems.at[seqs])
    copy.start()
    copies.append(copy)
    for copy in copies:
        copy.wait()


def shards(n_dp, n_tensor, n_z, *arrays):
    rows, width = arrays[0].shape
    seqs = arrays[4].shape[0]
    hbm = pl.BlockSpec(memory_space=pltpu.HBM)
    vmem = pl.BlockSpec(memory_space=pltpu.VMEM)
    arrays = [pltpu.with_memory_space_constraint(array, pltpu.HBM) for array in arrays]
    grad, margin = pl.pallas_call(
        functools.partial(stats_kernel, n_dp, n_tensor, n_z),
        out_shape=(
            pltpu.VMEM((rows, width), jnp.float32),
            pltpu.VMEM((seqs, LANES), jnp.float32),
        ),
        in_specs=[hbm] * 6,
        out_specs=(vmem, vmem),
        scratch_shapes=[
            pltpu.VMEM((rows, width), jnp.bfloat16),
            pltpu.VMEM((rows, width), jnp.bfloat16),
            pltpu.VMEM((2, rows), jnp.int32),
            pltpu.SMEM((2, seqs), jnp.int32),
            pltpu.VMEM((5, rows, LANES), jnp.float32),
            pltpu.VMEM((rows, LANES), jnp.int32),
            pltpu.VMEM((PARTS, LANES), jnp.float32),
            pltpu.VMEM((n_tensor, PARTS, LANES), jnp.float32),
            pltpu.VMEM((1, LANES), jnp.float32),
            pltpu.VMEM((n_dp, LANES), jnp.float32),
            pltpu.SemaphoreType.DMA((2, rows // GROUP)),
            pltpu.SemaphoreType.DMA((4,)),
            pltpu.SemaphoreType.DMA,
            pltpu.SemaphoreType.DMA,
            pltpu.SemaphoreType.DMA,
            pltpu.SemaphoreType.DMA,
            pltpu.SemaphoreType.REGULAR((3,)),
        ],
        compiler_params=pltpu.CompilerParams(
            collective_id=0, has_side_effects=True, vmem_limit_bytes=32 * 1024 * 1024
        ),
        name="row_stats",
    )(*arrays)
    return pl.pallas_call(
        scale_kernel,
        out_shape=(
            jax.ShapeDtypeStruct((rows, width), jnp.float32),
            jax.ShapeDtypeStruct((seqs,), jnp.float32),
        ),
        in_specs=[vmem, vmem],
        out_specs=(hbm, hbm),
        scratch_shapes=[
            pltpu.VMEM((rows, width), jnp.float32),
            pltpu.VMEM((seqs,), jnp.float32),
            pltpu.SemaphoreType.DMA((seqs + 1,)),
        ],
        compiler_params=pltpu.CompilerParams(vmem_limit_bytes=32 * 1024 * 1024),
        name="scale_grad",
    )(grad, margin)


def solution(mesh):
    n_dp, n_tensor = mesh.shape["dp"], mesh.shape["tensor"]
    n_z = 8 if n_dp % 8 == 0 and n_dp > 8 else n_dp // 2
    return jax.shard_map(
        functools.partial(shards, n_dp, n_tensor, n_z),
        mesh=mesh,
        in_specs=(P("dp", "tensor"), P("dp", "tensor"), P("dp"), P("dp"), P("dp"), P("dp")),
        out_specs=(P("dp", "tensor"), P("dp")),
        check_vma=False,
    )
```

```python
import functools
import jax
import jax.numpy as jnp
from jax import lax
from jax.experimental import pallas as pl
from jax.experimental.pallas import tpu as pltpu
from jax.sharding import PartitionSpec as P

beta_scale = 0.5
kl_scale = 0.25
MESH = pl.DeviceIdType.MESH
LANES = 128
CHUNK = 16
GROUP = 32
WAYS = 4
PARTS = 4
CORES = 2


def ring(size):
    return sorted(range(1, size), key=lambda k: -min(k, size - k))


def stats_kernel(
    n_dp,
    n_tensor,
    n_z,
    p_hbm,
    r_hbm,
    targets_hbm,
    mask_hbm,
    partner_hbm,
    chosen_hbm,
    grad_ref,
    margin_ref,
    p_buf,
    r_buf,
    rows_int,
    ids,
    lane_stats,
    hit_set,
    own_rows,
    all_rows,
    own_seqs,
    all_seqs,
    group_sems,
    small_sems,
    row_send,
    row_recv,
    seq_send,
    seq_recv,
    known_sems,
):
    rows, width = p_buf.shape
    tiles = width // LANES
    chunks = rows // CHUNK
    seqs = partner_hbm.shape[0]
    length = rows // seqs
    n_x = n_dp // n_z
    my_dp = lax.axis_index("dp")
    my_tensor = lax.axis_index("tensor")
    my_x = my_dp // n_z
    my_z = lax.rem(my_dp, n_z)

    my_y = my_tensor // CORES
    my_core = lax.rem(my_tensor, CORES)
    n_y = n_tensor // CORES
    sibling = {"tensor": my_tensor + 1 - 2 * my_core}

    def y_peer(y, core):
        return {"tensor": lax.rem(my_y + y, n_y) * CORES + core}

    def dp_peer(x, z):
        place = lax.rem(my_x + x, n_x) * n_z + lax.rem(my_z + z, n_z)
        return {"dp": place, "tensor": my_y * CORES + 1}

    def signal(sem, peer):
        pl.semaphore_signal(sem, inc=1, device_id=peer, device_id_type=MESH)

    small = [
        pltpu.make_async_copy(targets_hbm, rows_int.at[0], small_sems.at[0]),
        pltpu.make_async_copy(mask_hbm, rows_int.at[1], small_sems.at[1]),
        pltpu.make_async_copy(partner_hbm, ids.at[0], small_sems.at[2]),
        pltpu.make_async_copy(chosen_hbm, ids.at[1], small_sems.at[3]),
    ]
    def group_copies(c):
        here = pl.ds(pl.multiple_of(c * GROUP, GROUP), GROUP)
        return (
            pltpu.make_async_copy(p_hbm.at[here], p_buf.at[here], group_sems.at[0, c]),
            pltpu.make_async_copy(r_hbm.at[here], r_buf.at[here], group_sems.at[1, c]),
        )

    barrier = pltpu.get_barrier_semaphore()

    def greet_y():
        signal(barrier, sibling)
        for y in ring(n_y):
            signal(barrier, y_peer(y, 0))

    def greet_dp():
        for z in ring(n_z):
            signal(barrier, dp_peer(0, z))
        for x in ring(n_x):
            signal(barrier, dp_peer(x, 0))

    def read(*groups):
        for c in groups:
            for copy in group_copies(c):
                copy.start()

    read(0)
    small[0].start()
    greet_dp()
    read(1, 2, 3)
    greet_y()
    for copy in small[1:]:
        copy.start()

    small[0].wait()
    targets_row = (rows_int[0:1, :] - my_tensor * width).astype(jnp.float32)

    diagonal = (
        lax.broadcasted_iota(jnp.int32, (8, LANES), 1)
        - lax.broadcasted_iota(jnp.int32, (8, LANES), 0)
    )

    sub_c = lax.broadcasted_iota(jnp.int32, (CHUNK, LANES), 0)
    lane_c = lax.broadcasted_iota(jnp.int32, (CHUNK, LANES), 1)

    def peak_of(buf, here):
        tops = [buf[here, pl.ds(t * LANES, LANES)] for t in range(WAYS)]
        for t in range(WAYS, tiles):
            tops[t % WAYS] = jnp.maximum(tops[t % WAYS], buf[here, pl.ds(t * LANES, LANES)])
        return functools.reduce(jnp.maximum, tops).astype(jnp.float32)

    def sums_of(start):
        here = pl.ds(pl.multiple_of(start, CHUNK), CHUNK)
        top_p = peak_of(p_buf, here)
        top_r = peak_of(r_buf, here)
        peak_p = jnp.max(top_p, axis=1, keepdims=True)
        peak_r = jnp.max(top_r, axis=1, keepdims=True)
        scale_p = jnp.exp(top_p - peak_p)
        scale_r = jnp.exp(top_r - peak_r)
        own_target = jnp.where(lane_c == sub_c + start, targets_row, 0.0)
        hits = jnp.sum(own_target, axis=1, keepdims=True).astype(jnp.int32) - lane_c
        hit_set[here, :] = hits
        sum_p = jnp.zeros((CHUNK, LANES), jnp.float32)
        sum_r = sum_p
        cross = sum_p
        pick = sum_p
        for t in range(tiles):
            cols = pl.ds(t * LANES, LANES)
            p = p_buf[here, cols].astype(jnp.float32)
            r = r_buf[here, cols].astype(jnp.float32)
            e_p = jnp.exp(p - top_p)
            e_r = jnp.exp(r - top_r)
            gap = r - p
            sum_p += e_p
            sum_r += e_r
            cross += e_r * gap
            pick = jnp.where(hits == t * LANES, gap, pick)
        return sum_p * scale_p, sum_r * scale_r, cross * scale_r, pick, peak_p, peak_r

    def add_rows(acc, start, sums):
        total_p, total_r, cross, pick = [
            jnp.sum(part, axis=1, keepdims=True) for part in sums[:4]
        ]
        part_p = sums[4] + jnp.log(total_p)
        part_r = sums[5] + jnp.log(total_r)
        columns = (part_p, part_r, cross / total_r, pick)
        out = []
        for total, column in zip(acc, columns):
            for g in range(0, CHUNK, 8):
                total = total + jnp.where(diagonal == start + g, column[g : g + 8, :], 0.0)
            out.append(total)
        return tuple(out)

    def one_group(c, carry):
        acc, before = carry
        for copy in group_copies(c):
            copy.wait()
        for g in range(0, GROUP, CHUNK):
            start = c * GROUP + g
            sums = sums_of(start)
            acc = add_rows(acc, start - CHUNK, before)
            before = sums
        return acc, before

    ones = jnp.ones((CHUNK, LANES), jnp.float32)
    column = jnp.zeros((CHUNK, 1), jnp.float32)
    zero = jnp.zeros((8, LANES), jnp.float32)
    start = ((zero,) * PARTS, (ones, ones, ones, ones, column, column))
    acc, sums = lax.fori_loop(0, rows // GROUP, one_group, start)
    acc = add_rows(acc, rows - CHUNK, sums)

    for k in range(PARTS):
        own_rows[k : k + 1, :] = jnp.sum(acc[k], axis=0, keepdims=True)
    all_rows[my_tensor] = own_rows[...]

    @pl.when(my_core == 0)
    def _():
        pl.semaphore_wait(barrier, 2 * n_y - 1)

    @pl.when(my_core == 1)
    def _():
        pl.semaphore_wait(known_sems.at[0], 1)

    def send_rows(peer):
        pltpu.make_async_remote_copy(
            src_ref=own_rows,
            dst_ref=all_rows.at[my_tensor],
            send_sem=row_send,
            recv_sem=row_recv,
            device_id=peer,
            device_id_type=MESH,
        ).start()

    far_y, *near_y = ring(n_y)
    send_rows(y_peer(far_y, 1))
    send_rows(y_peer(far_y, 0))

    @pl.when(my_core == 0)
    def _():
        signal(known_sems.at[0], sibling)

    for y in near_y:
        send_rows(y_peer(y, 1))
        send_rows(y_peer(y, 0))
    send_rows(sibling)

    @pl.when(my_core == 1)
    def _():
        pl.semaphore_wait(barrier, 2 * (n_z + n_x) - 3)
        for x in ring(n_x):
            signal(known_sems.at[1], dp_peer(x, 0))
        pl.semaphore_wait(known_sems.at[1], n_x - 1)
        signal(known_sems.at[2], sibling)

    @pl.when(my_core == 0)
    def _():
        pl.semaphore_wait(known_sems.at[2], 1)

    for copy in small[1:]:
        copy.wait()
    mask_row = rows_int[1:2, :].astype(jnp.float32)
    sub_r = lax.broadcasted_iota(jnp.int32, (LANES, LANES), 0)
    mask_col = jnp.where(sub_r == 0, mask_row, 0.0).T[:, 0:1]

    sub_s = lax.broadcasted_iota(jnp.int32, (seqs, LANES), 0)
    lane_s = lax.broadcasted_iota(jnp.int32, (seqs, LANES), 1)
    place_col = jnp.zeros((seqs, LANES), jnp.int32)
    chosen_col = jnp.zeros((seqs, LANES), jnp.float32)
    for j in range(seqs):
        place_col = jnp.where(sub_s == j, lax.rem(ids[0, j], seqs) * length, place_col)
        chosen_col = jnp.where(sub_s == j, ids[1, j].astype(jnp.float32), chosen_col)
    sign_col = 2.0 * chosen_col - 1.0
    block_s = lane_s // length == sub_s

    others = all_rows.at[pl.ds(0, n_tensor - 1)]
    pltpu.make_async_copy(others, others, row_recv).wait()
    parts = [all_rows[k] for k in range(n_tensor)]
    peak = functools.reduce(jnp.maximum, parts)
    weights = [jnp.exp(part - peak) for part in parts]
    total = functools.reduce(jnp.add, weights)
    norm = peak + jnp.log(total)
    cross_row = functools.reduce(
        jnp.add, [w[1:2, :] * part[2:3, :] for w, part in zip(weights, parts)]
    )
    pick_row = functools.reduce(jnp.add, parts)[3:4, :]
    norm_p = norm[0:1, :]
    norm_r = norm[1:2, :]
    kl_row = cross_row / total[1:2, :] - norm_r + norm_p
    ratio_row = norm_r - norm_p - pick_row
    value_row = mask_row * (beta_scale * ratio_row + kl_scale * kl_row)
    own_col = jnp.sum(jnp.where(block_s, value_row, 0.0), axis=1, keepdims=True)
    own = jnp.sum(jnp.where(block_s, own_col, 0.0), axis=0, keepdims=True)
    own_seqs[...] = own
    all_seqs[pl.ds(my_dp, 1), :] = own

    my_rank = my_z * n_x + my_x
    for k in range(n_dp - 1):
        rank = k + (k + n_dp - my_rank) // n_dp
        pltpu.make_async_remote_copy(
            src_ref=own_seqs,
            dst_ref=all_seqs.at[pl.ds(my_dp, 1)],
            send_sem=seq_send,
            recv_sem=seq_recv,
            device_id={"dp": lax.rem(rank, n_x) * n_z + rank // n_x},
            device_id_type=MESH,
        ).start()

    stacked = jnp.where(sub_r == 0, norm_p, jnp.where(sub_r == 1, norm_r, 0.0))
    columns = stacked.T
    chosen_rows = jnp.concatenate(
        [jnp.broadcast_to(chosen_col[j : j + 1, :], (length, LANES)) for j in range(seqs)], axis=0
    )
    coef_hit = mask_col * (beta_scale * (2.0 * chosen_rows - 1.0))
    coef_kl = mask_col * (-kl_scale * (1.0 - chosen_rows))
    lane_stats[0] = jnp.broadcast_to(columns[:, 0:1], (LANES, LANES))
    lane_stats[1] = jnp.broadcast_to(columns[:, 1:2], (LANES, LANES))
    lane_stats[2] = coef_kl - coef_hit
    lane_stats[3] = coef_kl
    lane_stats[4] = coef_hit

    def grad_chunk(c, carry):
        here = pl.ds(pl.multiple_of(c * CHUNK, CHUNK), CHUNK)
        hits = hit_set[here, :]
        base_p = lane_stats[0, here, :]
        base_r = lane_stats[1, here, :]
        scale_p = lane_stats[2, here, :]
        scale_r = lane_stats[3, here, :]
        scale_hit = lane_stats[4, here, :]
        for t in range(tiles):
            cols = pl.ds(t * LANES, LANES)
            p = p_buf[here, cols].astype(jnp.float32)
            r = r_buf[here, cols].astype(jnp.float32)
            grad_ref[here, cols] = (
                jnp.exp(p - base_p) * scale_p
                - jnp.exp(r - base_r) * scale_r
                + jnp.where(hits == t * LANES, scale_hit, 0.0)
            )
        return carry

    lax.fori_loop(0, chunks, grad_chunk, 0)

    pltpu.make_async_copy(others, others, row_send).wait()
    others = all_seqs.at[pl.ds(0, n_dp - 1)]
    pltpu.make_async_copy(others, others, seq_send).wait()
    pltpu.make_async_copy(others, others, seq_recv).wait()
    partner_rows = jnp.zeros((seqs, LANES), jnp.float32)
    for j in range(seqs):
        row = all_seqs[pl.ds(ids[0, j] // seqs, 1), :]
        partner_rows = jnp.where(sub_s == j, row, partner_rows)
    partner_value = jnp.sum(
        jnp.where(lane_s == place_col, partner_rows, 0.0), axis=1, keepdims=True
    )
    margin_ref[...] = sign_col * (own_col - partner_value)


def scale_kernel(grad_ref, margin_ref, out_hbm, loss_hbm, out_buf, loss_buf, sems):
    rows, width = out_buf.shape
    seqs = margin_ref.shape[0]
    length = rows // seqs
    margin = margin_ref[...]
    slope = -jax.nn.sigmoid(-margin)
    copies = []
    for j in range(seqs):
        here = pl.ds(j * length, length)
        out_buf[here, :] = grad_ref[here, :] * slope[j : j + 1, 0:1]
        copy = pltpu.make_async_copy(out_buf.at[here], out_hbm.at[here], sems.at[j])
        copy.start()
        copies.append(copy)
    loss = jnp.maximum(-margin, 0.0) + jnp.log1p(jnp.exp(-jnp.abs(margin)))
    sub = lax.broadcasted_iota(jnp.int32, (seqs, LANES), 0)
    lane = lax.broadcasted_iota(jnp.int32, (seqs, LANES), 1)
    loss_buf[...] = jnp.sum(jnp.where(sub == lane, loss, 0.0), axis=0)[:seqs]
    copy = pltpu.make_async_copy(loss_buf, loss_hbm, sems.at[seqs])
    copy.start()
    copies.append(copy)
    for copy in copies:
        copy.wait()


def shards(n_dp, n_tensor, n_z, *arrays):
    rows, width = arrays[0].shape
    seqs = arrays[4].shape[0]
    hbm = pl.BlockSpec(memory_space=pltpu.HBM)
    vmem = pl.BlockSpec(memory_space=pltpu.VMEM)
    arrays = [pltpu.with_memory_space_constraint(array, pltpu.HBM) for array in arrays]
    grad, margin = pl.pallas_call(
        functools.partial(stats_kernel, n_dp, n_tensor, n_z),
        out_shape=(
            pltpu.VMEM((rows, width), jnp.float32),
            pltpu.VMEM((seqs, LANES), jnp.float32),
        ),
        in_specs=[hbm] * 6,
        out_specs=(vmem, vmem),
        scratch_shapes=[
            pltpu.VMEM((rows, width), jnp.bfloat16),
            pltpu.VMEM((rows, width), jnp.bfloat16),
            pltpu.VMEM((2, rows), jnp.int32),
            pltpu.SMEM((2, seqs), jnp.int32),
            pltpu.VMEM((5, rows, LANES), jnp.float32),
            pltpu.VMEM((rows, LANES), jnp.int32),
            pltpu.VMEM((PARTS, LANES), jnp.float32),
            pltpu.VMEM((n_tensor, PARTS, LANES), jnp.float32),
            pltpu.VMEM((1, LANES), jnp.float32),
            pltpu.VMEM((n_dp, LANES), jnp.float32),
            pltpu.SemaphoreType.DMA((2, rows // GROUP)),
            pltpu.SemaphoreType.DMA((4,)),
            pltpu.SemaphoreType.DMA,
            pltpu.SemaphoreType.DMA,
            pltpu.SemaphoreType.DMA,
            pltpu.SemaphoreType.DMA,
            pltpu.SemaphoreType.REGULAR((3,)),
        ],
        compiler_params=pltpu.CompilerParams(
            collective_id=0, has_side_effects=True, vmem_limit_bytes=32 * 1024 * 1024
        ),
        name="row_stats",
    )(*arrays)
    return pl.pallas_call(
        scale_kernel,
        out_shape=(
            jax.ShapeDtypeStruct((rows, width), jnp.float32),
            jax.ShapeDtypeStruct((seqs,), jnp.float32),
        ),
        in_specs=[vmem, vmem],
        out_specs=(hbm, hbm),
        scratch_shapes=[
            pltpu.VMEM((rows, width), jnp.float32),
            pltpu.VMEM((seqs,), jnp.float32),
            pltpu.SemaphoreType.DMA((seqs + 1,)),
        ],
        compiler_params=pltpu.CompilerParams(vmem_limit_bytes=32 * 1024 * 1024),
        name="scale_grad",
    )(grad, margin)


def solution(mesh):
    n_dp, n_tensor = mesh.shape["dp"], mesh.shape["tensor"]
    n_z = 8 if n_dp % 8 == 0 and n_dp > 8 else n_dp // 2
    return jax.shard_map(
        functools.partial(shards, n_dp, n_tensor, n_z),
        mesh=mesh,
        in_specs=(P("dp", "tensor"), P("dp", "tensor"), P("dp"), P("dp"), P("dp"), P("dp")),
        out_specs=(P("dp", "tensor"), P("dp")),
        check_vma=False,
    )
```

```python
import functools
import jax
import jax.numpy as jnp
from jax import lax
from jax.experimental import pallas as pl
from jax.experimental.pallas import tpu as pltpu
from jax.sharding import PartitionSpec as P

beta_scale = 0.5
kl_scale = 0.25
MESH = pl.DeviceIdType.MESH
LANES = 128
CHUNK = 32
GROUP = 32
WAYS = 4
PARTS = 4
CORES = 2


def ring(size):
    return sorted(range(1, size), key=lambda k: -min(k, size - k))


def tree(combine, items):
    while len(items) > 1:
        items = [combine(*items[k : k + 2]) if k + 1 < len(items) else items[k] for k in range(0, len(items), 2)]
    return items[0]


def stats_kernel(
    n_dp,
    n_tensor,
    n_z,
    p_hbm,
    r_hbm,
    targets_hbm,
    mask_hbm,
    partner_hbm,
    chosen_hbm,
    grad_ref,
    margin_ref,
    p_buf,
    r_buf,
    rows_int,
    ids,
    lane_stats,
    hit_set,
    own_rows,
    all_rows,
    own_seqs,
    all_seqs,
    group_sems,
    small_sems,
    row_send,
    row_recv,
    seq_send,
    seq_recv,
    known_sems,
):
    rows, width = p_buf.shape
    tiles = width // LANES
    chunks = rows // CHUNK
    seqs = partner_hbm.shape[0]
    length = rows // seqs
    n_x = n_dp // n_z
    my_dp = lax.axis_index("dp")
    my_tensor = lax.axis_index("tensor")
    my_x = my_dp // n_z
    my_z = lax.rem(my_dp, n_z)

    my_y = my_tensor // CORES
    my_core = lax.rem(my_tensor, CORES)
    n_y = n_tensor // CORES
    sibling = {"tensor": my_tensor + 1 - 2 * my_core}

    def y_peer(y, core):
        return {"tensor": lax.rem(my_y + y, n_y) * CORES + core}

    def dp_peer(x, z):
        place = lax.rem(my_x + x, n_x) * n_z + lax.rem(my_z + z, n_z)
        return {"dp": place, "tensor": my_y * CORES + 1}

    def signal(sem, peer):
        pl.semaphore_signal(sem, inc=1, device_id=peer, device_id_type=MESH)

    small = [
        pltpu.make_async_copy(targets_hbm, rows_int.at[0], small_sems.at[0]),
        pltpu.make_async_copy(mask_hbm, rows_int.at[1], small_sems.at[1]),
        pltpu.make_async_copy(partner_hbm, ids.at[0], small_sems.at[2]),
        pltpu.make_async_copy(chosen_hbm, ids.at[1], small_sems.at[3]),
    ]
    def group_copies(c):
        here = pl.ds(pl.multiple_of(c * GROUP, GROUP), GROUP)
        return (
            pltpu.make_async_copy(p_hbm.at[here], p_buf.at[here], group_sems.at[0, c]),
            pltpu.make_async_copy(r_hbm.at[here], r_buf.at[here], group_sems.at[1, c]),
        )

    barrier = pltpu.get_barrier_semaphore()

    def greet_y():
        signal(barrier, sibling)
        for y in ring(n_y):
            signal(barrier, y_peer(y, 0))

    def greet_dp():
        for z in ring(n_z):
            signal(barrier, dp_peer(0, z))
        for x in ring(n_x):
            signal(barrier, dp_peer(x, 0))

    def read(*groups):
        for c in groups:
            for copy in group_copies(c):
                copy.start()

    read(0)
    small[0].start()
    greet_dp()
    read(1, 2, 3)
    greet_y()

    small[0].wait()
    targets_row = (rows_int[0:1, :] - my_tensor * width).astype(jnp.float32)

    diagonal = (
        lax.broadcasted_iota(jnp.int32, (8, LANES), 1)
        - lax.broadcasted_iota(jnp.int32, (8, LANES), 0)
    )

    sub_c = lax.broadcasted_iota(jnp.int32, (CHUNK, LANES), 0)
    lane_c = lax.broadcasted_iota(jnp.int32, (CHUNK, LANES), 1)

    def peak_of(buf, here):
        tops = [buf[here, pl.ds(t * LANES, LANES)] for t in range(WAYS)]
        for t in range(WAYS, tiles):
            tops[t % WAYS] = jnp.maximum(tops[t % WAYS], buf[here, pl.ds(t * LANES, LANES)])
        return functools.reduce(jnp.maximum, tops).astype(jnp.float32)

    def sums_of(start):
        here = pl.ds(pl.multiple_of(start, CHUNK), CHUNK)
        top_p = peak_of(p_buf, here)
        top_r = peak_of(r_buf, here)
        peak_p = jnp.max(top_p, axis=1, keepdims=True)
        peak_r = jnp.max(top_r, axis=1, keepdims=True)
        scale_p = jnp.exp(top_p - peak_p)
        scale_r = jnp.exp(top_r - peak_r)
        own_target = jnp.where(lane_c == sub_c + start, targets_row, 0.0)
        hits = jnp.sum(own_target, axis=1, keepdims=True).astype(jnp.int32) - lane_c
        hit_set[here, :] = hits
        sum_p = jnp.zeros((CHUNK, LANES), jnp.float32)
        sum_r = sum_p
        cross = sum_p
        pick = sum_p
        for t in range(tiles):
            cols = pl.ds(t * LANES, LANES)
            p = p_buf[here, cols].astype(jnp.float32)
            r = r_buf[here, cols].astype(jnp.float32)
            e_p = jnp.exp(p - top_p)
            e_r = jnp.exp(r - top_r)
            gap = r - p
            sum_p += e_p
            sum_r += e_r
            cross += e_r * gap
            pick = jnp.where(hits == t * LANES, gap, pick)
        return sum_p * scale_p, sum_r * scale_r, cross * scale_r, pick, peak_p, peak_r

    def add_rows(acc, start, sums):
        total_p, total_r, cross, pick = [
            jnp.sum(part, axis=1, keepdims=True) for part in sums[:4]
        ]
        part_p = sums[4] + jnp.log(total_p)
        part_r = sums[5] + jnp.log(total_r)
        columns = (part_p, part_r, cross / total_r, pick)
        out = []
        for total, column in zip(acc, columns):
            for g in range(0, CHUNK, 8):
                total = total + jnp.where(diagonal == start + g, column[g : g + 8, :], 0.0)
            out.append(total)
        return tuple(out)

    def one_group(c, carry):
        acc, before = carry
        for copy in group_copies(c):
            copy.wait()
        for g in range(0, GROUP, CHUNK):
            start = c * GROUP + g
            sums = sums_of(start)
            acc = add_rows(acc, start - CHUNK, before)
            before = sums
        return acc, before

    ones = jnp.ones((CHUNK, LANES), jnp.float32)
    column = jnp.zeros((CHUNK, 1), jnp.float32)
    zero = jnp.zeros((8, LANES), jnp.float32)
    start = ((zero,) * PARTS, (ones, ones, ones, ones, column, column))
    acc, sums = lax.fori_loop(0, rows // GROUP, one_group, start)
    acc = add_rows(acc, rows - CHUNK, sums)

    for k in range(PARTS):
        own_rows[k : k + 1, :] = jnp.sum(acc[k], axis=0, keepdims=True)
    all_rows[my_tensor] = own_rows[...]

    @pl.when(my_core == 0)
    def _():
        pl.semaphore_wait(barrier, 2 * n_y - 1)

    @pl.when(my_core == 1)
    def _():
        pl.semaphore_wait(known_sems.at[0], 1)

    def send_rows(peer):
        pltpu.make_async_remote_copy(
            src_ref=own_rows,
            dst_ref=all_rows.at[my_tensor],
            send_sem=row_send,
            recv_sem=row_recv,
            device_id=peer,
            device_id_type=MESH,
        ).start()

    far_y, *near_y = ring(n_y)
    send_rows(y_peer(far_y, 1))
    send_rows(y_peer(far_y, 0))

    @pl.when(my_core == 0)
    def _():
        signal(known_sems.at[0], sibling)

    for y in near_y:
        send_rows(y_peer(y, 1))
        send_rows(y_peer(y, 0))
    send_rows(sibling)

    for copy in small[1:]:
        copy.start()

    @pl.when(my_core == 1)
    def _():
        pl.semaphore_wait(barrier, 2 * (n_z + n_x) - 3)
        for x in ring(n_x):
            signal(known_sems.at[1], dp_peer(x, 0))
        pl.semaphore_wait(known_sems.at[1], n_x - 1)
        signal(known_sems.at[2], sibling)

    @pl.when(my_core == 0)
    def _():
        pl.semaphore_wait(known_sems.at[2], 1)

    for copy in small[1:]:
        copy.wait()
    mask_row = rows_int[1:2, :].astype(jnp.float32)
    sub_r = lax.broadcasted_iota(jnp.int32, (LANES, LANES), 0)
    mask_col = jnp.where(sub_r == 0, mask_row, 0.0).T[:, 0:1]

    sub_s = lax.broadcasted_iota(jnp.int32, (seqs, LANES), 0)
    lane_s = lax.broadcasted_iota(jnp.int32, (seqs, LANES), 1)
    place_col = jnp.zeros((seqs, LANES), jnp.int32)
    chosen_col = jnp.zeros((seqs, LANES), jnp.float32)
    for j in range(seqs):
        place_col = jnp.where(sub_s == j, lax.rem(ids[0, j], seqs) * length, place_col)
        chosen_col = jnp.where(sub_s == j, ids[1, j].astype(jnp.float32), chosen_col)
    sign_col = 2.0 * chosen_col - 1.0
    block_s = lane_s // length == sub_s

    others = all_rows.at[pl.ds(0, n_tensor - 1)]
    pltpu.make_async_copy(others, others, row_recv).wait()
    parts = [all_rows[k] for k in range(n_tensor)]
    peak = tree(jnp.maximum, parts)
    weights = [jnp.exp(part - peak) for part in parts]
    total = tree(jnp.add, weights)
    norm = peak + jnp.log(total)
    cross_row = tree(
        jnp.add, [w[1:2, :] * part[2:3, :] for w, part in zip(weights, parts)]
    )
    pick_row = tree(jnp.add, parts)[3:4, :]
    norm_p = norm[0:1, :]
    norm_r = norm[1:2, :]
    kl_row = cross_row / total[1:2, :] - norm_r + norm_p
    ratio_row = norm_r - norm_p - pick_row
    value_row = mask_row * (beta_scale * ratio_row + kl_scale * kl_row)
    own_col = jnp.sum(jnp.where(block_s, value_row, 0.0), axis=1, keepdims=True)
    own = jnp.sum(jnp.where(block_s, own_col, 0.0), axis=0, keepdims=True)
    own_seqs[...] = own
    all_seqs[pl.ds(my_dp, 1), :] = own

    my_rank = my_z * n_x + my_x
    for k in range(n_dp - 1):
        rank = k + (k + n_dp - my_rank) // n_dp
        pltpu.make_async_remote_copy(
            src_ref=own_seqs,
            dst_ref=all_seqs.at[pl.ds(my_dp, 1)],
            send_sem=seq_send,
            recv_sem=seq_recv,
            device_id={"dp": lax.rem(rank, n_x) * n_z + rank // n_x},
            device_id_type=MESH,
        ).start()

    stacked = jnp.where(sub_r == 0, norm_p, jnp.where(sub_r == 1, norm_r, 0.0))
    columns = stacked.T
    chosen_rows = jnp.concatenate(
        [jnp.broadcast_to(chosen_col[j : j + 1, :], (length, LANES)) for j in range(seqs)], axis=0
    )
    coef_hit = mask_col * (beta_scale * (2.0 * chosen_rows - 1.0))
    coef_kl = mask_col * (-kl_scale * (1.0 - chosen_rows))
    lane_stats[0] = jnp.broadcast_to(columns[:, 0:1], (LANES, LANES))
    lane_stats[1] = jnp.broadcast_to(columns[:, 1:2], (LANES, LANES))
    lane_stats[2] = coef_kl - coef_hit
    lane_stats[3] = coef_kl
    lane_stats[4] = coef_hit

    def grad_chunk(c, carry):
        here = pl.ds(pl.multiple_of(c * CHUNK, CHUNK), CHUNK)
        hits = hit_set[here, :]
        base_p = lane_stats[0, here, :]
        base_r = lane_stats[1, here, :]
        scale_p = lane_stats[2, here, :]
        scale_r = lane_stats[3, here, :]
        scale_hit = lane_stats[4, here, :]
        for t in range(tiles):
            cols = pl.ds(t * LANES, LANES)
            p = p_buf[here, cols].astype(jnp.float32)
            r = r_buf[here, cols].astype(jnp.float32)
            grad_ref[here, cols] = (
                jnp.exp(p - base_p) * scale_p
                - jnp.exp(r - base_r) * scale_r
                + jnp.where(hits == t * LANES, scale_hit, 0.0)
            )
        return carry

    lax.fori_loop(0, chunks, grad_chunk, 0)

    others_dp = all_seqs.at[pl.ds(0, n_dp - 1)]
    pltpu.make_async_copy(others_dp, others_dp, seq_recv).wait()
    partner_rows = jnp.zeros((seqs, LANES), jnp.float32)
    for j in range(seqs):
        row = all_seqs[pl.ds(ids[0, j] // seqs, 1), :]
        partner_rows = jnp.where(sub_s == j, row, partner_rows)
    partner_value = jnp.sum(
        jnp.where(lane_s == place_col, partner_rows, 0.0), axis=1, keepdims=True
    )
    margin_ref[...] = sign_col * (own_col - partner_value)
    pltpu.make_async_copy(others, others, row_send).wait()
    pltpu.make_async_copy(others_dp, others_dp, seq_send).wait()


def scale_kernel(grad_ref, margin_ref, out_hbm, loss_hbm, out_buf, loss_buf, sems):
    rows, width = out_buf.shape
    seqs = margin_ref.shape[0]
    length = rows // seqs
    margin = margin_ref[...]
    slope = -jax.nn.sigmoid(-margin)
    copies = []
    for j in range(seqs):
        here = pl.ds(j * length, length)
        out_buf[here, :] = grad_ref[here, :] * slope[j : j + 1, 0:1]
        copy = pltpu.make_async_copy(out_buf.at[here], out_hbm.at[here], sems.at[j])
        copy.start()
        copies.append(copy)
    loss = jnp.maximum(-margin, 0.0) + jnp.log1p(jnp.exp(-jnp.abs(margin)))
    sub = lax.broadcasted_iota(jnp.int32, (seqs, LANES), 0)
    lane = lax.broadcasted_iota(jnp.int32, (seqs, LANES), 1)
    loss_buf[...] = jnp.sum(jnp.where(sub == lane, loss, 0.0), axis=0)[:seqs]
    copy = pltpu.make_async_copy(loss_buf, loss_hbm, sems.at[seqs])
    copy.start()
    copies.append(copy)
    for copy in copies:
        copy.wait()


def shards(n_dp, n_tensor, n_z, *arrays):
    rows, width = arrays[0].shape
    seqs = arrays[4].shape[0]
    hbm = pl.BlockSpec(memory_space=pltpu.HBM)
    vmem = pl.BlockSpec(memory_space=pltpu.VMEM)
    arrays = [pltpu.with_memory_space_constraint(array, pltpu.HBM) for array in arrays]
    grad, margin = pl.pallas_call(
        functools.partial(stats_kernel, n_dp, n_tensor, n_z),
        out_shape=(
            pltpu.VMEM((rows, width), jnp.float32),
            pltpu.VMEM((seqs, LANES), jnp.float32),
        ),
        in_specs=[hbm] * 6,
        out_specs=(vmem, vmem),
        scratch_shapes=[
            pltpu.VMEM((rows, width), jnp.bfloat16),
            pltpu.VMEM((rows, width), jnp.bfloat16),
            pltpu.VMEM((2, rows), jnp.int32),
            pltpu.SMEM((2, seqs), jnp.int32),
            pltpu.VMEM((5, rows, LANES), jnp.float32),
            pltpu.VMEM((rows, LANES), jnp.int32),
            pltpu.VMEM((PARTS, LANES), jnp.float32),
            pltpu.VMEM((n_tensor, PARTS, LANES), jnp.float32),
            pltpu.VMEM((1, LANES), jnp.float32),
            pltpu.VMEM((n_dp, LANES), jnp.float32),
            pltpu.SemaphoreType.DMA((2, rows // GROUP)),
            pltpu.SemaphoreType.DMA((4,)),
            pltpu.SemaphoreType.DMA,
            pltpu.SemaphoreType.DMA,
            pltpu.SemaphoreType.DMA,
            pltpu.SemaphoreType.DMA,
            pltpu.SemaphoreType.REGULAR((3,)),
        ],
        compiler_params=pltpu.CompilerParams(
            collective_id=0, has_side_effects=True, vmem_limit_bytes=32 * 1024 * 1024
        ),
        name="row_stats",
    )(*arrays)
    return pl.pallas_call(
        scale_kernel,
        out_shape=(
            jax.ShapeDtypeStruct((rows, width), jnp.float32),
            jax.ShapeDtypeStruct((seqs,), jnp.float32),
        ),
        in_specs=[vmem, vmem],
        out_specs=(hbm, hbm),
        scratch_shapes=[
            pltpu.VMEM((rows, width), jnp.float32),
            pltpu.VMEM((seqs,), jnp.float32),
            pltpu.SemaphoreType.DMA((seqs + 1,)),
        ],
        compiler_params=pltpu.CompilerParams(vmem_limit_bytes=32 * 1024 * 1024),
        name="scale_grad",
    )(grad, margin)


def solution(mesh):
    n_dp, n_tensor = mesh.shape["dp"], mesh.shape["tensor"]
    n_z = 8 if n_dp % 8 == 0 and n_dp > 8 else n_dp // 2
    return jax.shard_map(
        functools.partial(shards, n_dp, n_tensor, n_z),
        mesh=mesh,
        in_specs=(P("dp", "tensor"), P("dp", "tensor"), P("dp"), P("dp"), P("dp"), P("dp")),
        out_specs=(P("dp", "tensor"), P("dp")),
        check_vma=False,
    )
```

```python
import functools
import jax
import jax.numpy as jnp
from jax import lax
from jax.experimental import pallas as pl
from jax.experimental.pallas import tpu as pltpu
from jax.sharding import PartitionSpec as P

beta_scale = 0.5
kl_scale = 0.25
MESH = pl.DeviceIdType.MESH
LANES = 128
CHUNK = 32
GROUP = 32
WAYS = 4
PARTS = 4
CORES = 2


def ring(size):
    return sorted(range(1, size), key=lambda k: -min(k, size - k))


def tree(combine, items):
    while len(items) > 1:
        items = [combine(*items[k : k + 2]) if k + 1 < len(items) else items[k] for k in range(0, len(items), 2)]
    return items[0]


def stats_kernel(
    n_dp,
    n_tensor,
    n_z,
    p_hbm,
    r_hbm,
    targets_hbm,
    mask_hbm,
    partner_hbm,
    chosen_hbm,
    grad_ref,
    margin_ref,
    p_buf,
    r_buf,
    rows_int,
    ids,
    lane_stats,
    hit_set,
    own_rows,
    all_rows,
    own_seqs,
    all_seqs,
    group_sems,
    small_sems,
    row_send,
    row_recv,
    seq_send,
    seq_recv,
    known_sems,
):
    rows, width = p_buf.shape
    tiles = width // LANES
    chunks = rows // CHUNK
    seqs = partner_hbm.shape[0]
    length = rows // seqs
    n_x = n_dp // n_z
    my_dp = lax.axis_index("dp")
    my_tensor = lax.axis_index("tensor")
    my_x = my_dp // n_z
    my_z = lax.rem(my_dp, n_z)

    my_y = my_tensor // CORES
    my_core = lax.rem(my_tensor, CORES)
    n_y = n_tensor // CORES
    sibling = {"tensor": my_tensor + 1 - 2 * my_core}

    def y_peer(y, core):
        return {"tensor": lax.rem(my_y + y, n_y) * CORES + core}

    def dp_peer(x, z):
        place = lax.rem(my_x + x, n_x) * n_z + lax.rem(my_z + z, n_z)
        return {"dp": place, "tensor": my_y * CORES + 1}

    def signal(sem, peer):
        pl.semaphore_signal(sem, inc=1, device_id=peer, device_id_type=MESH)

    small = [
        pltpu.make_async_copy(targets_hbm, rows_int.at[0], small_sems.at[0]),
        pltpu.make_async_copy(mask_hbm, rows_int.at[1], small_sems.at[1]),
        pltpu.make_async_copy(partner_hbm, ids.at[0], small_sems.at[2]),
        pltpu.make_async_copy(chosen_hbm, ids.at[1], small_sems.at[3]),
    ]
    def group_copies(c):
        here = pl.ds(pl.multiple_of(c * GROUP, GROUP), GROUP)
        return (
            pltpu.make_async_copy(p_hbm.at[here], p_buf.at[here], group_sems.at[0, c]),
            pltpu.make_async_copy(r_hbm.at[here], r_buf.at[here], group_sems.at[1, c]),
        )

    barrier = pltpu.get_barrier_semaphore()

    def greet_y():
        signal(barrier, sibling)
        for y in ring(n_y):
            signal(barrier, y_peer(y, 0))

    def greet_dp():
        for z in ring(n_z):
            signal(barrier, dp_peer(0, z))
        for x in ring(n_x):
            signal(barrier, dp_peer(x, 0))

    def read(*groups):
        for c in groups:
            for copy in group_copies(c):
                copy.start()

    small[0].start()
    read(0, 1, 2, 3)
    greet_dp()
    greet_y()

    small[0].wait()
    targets_row = (rows_int[0:1, :] - my_tensor * width).astype(jnp.float32)

    diagonal = (
        lax.broadcasted_iota(jnp.int32, (8, LANES), 1)
        - lax.broadcasted_iota(jnp.int32, (8, LANES), 0)
    )

    sub_c = lax.broadcasted_iota(jnp.int32, (CHUNK, LANES), 0)
    lane_c = lax.broadcasted_iota(jnp.int32, (CHUNK, LANES), 1)

    def peak_of(buf, here):
        tops = [buf[here, pl.ds(t * LANES, LANES)] for t in range(WAYS)]
        for t in range(WAYS, tiles):
            tops[t % WAYS] = jnp.maximum(tops[t % WAYS], buf[here, pl.ds(t * LANES, LANES)])
        return functools.reduce(jnp.maximum, tops).astype(jnp.float32)

    def sums_of(start):
        here = pl.ds(pl.multiple_of(start, CHUNK), CHUNK)
        top_p = peak_of(p_buf, here)
        top_r = peak_of(r_buf, here)
        peak_p = jnp.max(top_p, axis=1, keepdims=True)
        peak_r = jnp.max(top_r, axis=1, keepdims=True)
        scale_p = jnp.exp(top_p - peak_p)
        scale_r = jnp.exp(top_r - peak_r)
        own_target = jnp.where(lane_c == sub_c + start, targets_row, 0.0)
        hits = jnp.sum(own_target, axis=1, keepdims=True).astype(jnp.int32) - lane_c
        hit_set[here, :] = hits
        sum_p = jnp.zeros((CHUNK, LANES), jnp.float32)
        sum_r = sum_p
        cross = sum_p
        pick = sum_p
        for t in range(tiles):
            cols = pl.ds(t * LANES, LANES)
            p = p_buf[here, cols].astype(jnp.float32)
            r = r_buf[here, cols].astype(jnp.float32)
            e_p = jnp.exp(p - top_p)
            e_r = jnp.exp(r - top_r)
            gap = r - p
            sum_p += e_p
            sum_r += e_r
            cross += e_r * gap
            pick = jnp.where(hits == t * LANES, gap, pick)
        return sum_p * scale_p, sum_r * scale_r, cross * scale_r, pick, peak_p, peak_r

    def add_rows(acc, start, sums):
        total_p, total_r, cross, pick = [
            jnp.sum(part, axis=1, keepdims=True) for part in sums[:4]
        ]
        part_p = sums[4] + jnp.log(total_p)
        part_r = sums[5] + jnp.log(total_r)
        columns = (part_p, part_r, cross / total_r, pick)
        out = []
        for total, column in zip(acc, columns):
            for g in range(0, CHUNK, 8):
                total = total + jnp.where(diagonal == start + g, column[g : g + 8, :], 0.0)
            out.append(total)
        return tuple(out)

    def one_group(c, carry):
        acc, before = carry
        for copy in group_copies(c):
            copy.wait()
        for g in range(0, GROUP, CHUNK):
            start = c * GROUP + g
            sums = sums_of(start)
            acc = add_rows(acc, start - CHUNK, before)
            before = sums
        return acc, before

    ones = jnp.ones((CHUNK, LANES), jnp.float32)
    column = jnp.zeros((CHUNK, 1), jnp.float32)
    zero = jnp.zeros((8, LANES), jnp.float32)
    start = ((zero,) * PARTS, (ones, ones, ones, ones, column, column))
    acc, sums = start
    for c in range(rows // GROUP):
        acc, sums = one_group(c, (acc, sums))
    acc = add_rows(acc, rows - CHUNK, sums)

    for k in range(PARTS):
        own_rows[k : k + 1, :] = jnp.sum(acc[k], axis=0, keepdims=True)
    all_rows[my_tensor] = own_rows[...]

    @pl.when(my_core == 0)
    def _():
        pl.semaphore_wait(barrier, 2 * n_y - 1)

    @pl.when(my_core == 1)
    def _():
        pl.semaphore_wait(known_sems.at[0], 1)

    def send_rows(peer):
        pltpu.make_async_remote_copy(
            src_ref=own_rows,
            dst_ref=all_rows.at[my_tensor],
            send_sem=row_send,
            recv_sem=row_recv,
            device_id=peer,
            device_id_type=MESH,
        ).start()

    far_y, *near_y = ring(n_y)
    send_rows(y_peer(far_y, 1))
    send_rows(y_peer(far_y, 0))

    @pl.when(my_core == 0)
    def _():
        signal(known_sems.at[0], sibling)

    for y in near_y:
        send_rows(y_peer(y, 1))
        send_rows(y_peer(y, 0))
    send_rows(sibling)

    for copy in small[1:]:
        copy.start()

    @pl.when(my_core == 1)
    def _():
        pl.semaphore_wait(barrier, 2 * (n_z + n_x) - 3)
        for x in ring(n_x):
            signal(known_sems.at[1], dp_peer(x, 0))
        pl.semaphore_wait(known_sems.at[1], n_x - 1)
        signal(known_sems.at[2], sibling)

    @pl.when(my_core == 0)
    def _():
        pl.semaphore_wait(known_sems.at[2], 1)

    for copy in small[1:]:
        copy.wait()
    mask_row = rows_int[1:2, :].astype(jnp.float32)
    sub_r = lax.broadcasted_iota(jnp.int32, (LANES, LANES), 0)
    mask_col = jnp.where(sub_r == 0, mask_row, 0.0).T[:, 0:1]

    sub_s = lax.broadcasted_iota(jnp.int32, (seqs, LANES), 0)
    lane_s = lax.broadcasted_iota(jnp.int32, (seqs, LANES), 1)
    place_col = jnp.zeros((seqs, LANES), jnp.int32)
    chosen_col = jnp.zeros((seqs, LANES), jnp.float32)
    for j in range(seqs):
        place_col = jnp.where(sub_s == j, lax.rem(ids[0, j], seqs) * length, place_col)
        chosen_col = jnp.where(sub_s == j, ids[1, j].astype(jnp.float32), chosen_col)
    sign_col = 2.0 * chosen_col - 1.0
    block_s = lane_s // length == sub_s

    others = all_rows.at[pl.ds(0, n_tensor - 1)]
    pltpu.make_async_copy(others, others, row_recv).wait()
    parts = [all_rows[k] for k in range(n_tensor)]
    peak = tree(jnp.maximum, parts)
    weights = [jnp.exp(part - peak) for part in parts]
    total = tree(jnp.add, weights)
    norm = peak + jnp.log(total)
    cross_row = tree(
        jnp.add, [w[1:2, :] * part[2:3, :] for w, part in zip(weights, parts)]
    )
    pick_row = tree(jnp.add, parts)[3:4, :]
    norm_p = norm[0:1, :]
    norm_r = norm[1:2, :]
    kl_row = cross_row / total[1:2, :] - norm_r + norm_p
    ratio_row = norm_r - norm_p - pick_row
    value_row = mask_row * (beta_scale * ratio_row + kl_scale * kl_row)
    own_col = jnp.sum(jnp.where(block_s, value_row, 0.0), axis=1, keepdims=True)
    own = jnp.sum(jnp.where(block_s, own_col, 0.0), axis=0, keepdims=True)
    own_seqs[...] = own
    all_seqs[pl.ds(my_dp, 1), :] = own

    my_rank = my_z * n_x + my_x
    for k in range(n_dp - 1):
        rank = k + (k + n_dp - my_rank) // n_dp
        pltpu.make_async_remote_copy(
            src_ref=own_seqs,
            dst_ref=all_seqs.at[pl.ds(my_dp, 1)],
            send_sem=seq_send,
            recv_sem=seq_recv,
            device_id={"dp": lax.rem(rank, n_x) * n_z + rank // n_x},
            device_id_type=MESH,
        ).start()

    stacked = jnp.where(sub_r == 0, norm_p, jnp.where(sub_r == 1, norm_r, 0.0))
    columns = stacked.T
    chosen_rows = jnp.concatenate(
        [jnp.broadcast_to(chosen_col[j : j + 1, :], (length, LANES)) for j in range(seqs)], axis=0
    )
    coef_hit = mask_col * (beta_scale * (2.0 * chosen_rows - 1.0))
    coef_kl = mask_col * (-kl_scale * (1.0 - chosen_rows))
    lane_stats[0] = jnp.broadcast_to(columns[:, 0:1], (LANES, LANES))
    lane_stats[1] = jnp.broadcast_to(columns[:, 1:2], (LANES, LANES))
    lane_stats[2] = coef_kl - coef_hit
    lane_stats[3] = coef_kl
    lane_stats[4] = coef_hit

    def grad_chunk(c, carry):
        here = pl.ds(pl.multiple_of(c * CHUNK, CHUNK), CHUNK)
        hits = hit_set[here, :]
        base_p = lane_stats[0, here, :]
        base_r = lane_stats[1, here, :]
        scale_p = lane_stats[2, here, :]
        scale_r = lane_stats[3, here, :]
        scale_hit = lane_stats[4, here, :]
        for t in range(tiles):
            cols = pl.ds(t * LANES, LANES)
            p = p_buf[here, cols].astype(jnp.float32)
            r = r_buf[here, cols].astype(jnp.float32)
            grad_ref[here, cols] = (
                jnp.exp(p - base_p) * scale_p
                - jnp.exp(r - base_r) * scale_r
                + jnp.where(hits == t * LANES, scale_hit, 0.0)
            )
        return carry

    lax.fori_loop(0, chunks, grad_chunk, 0)

    others_dp = all_seqs.at[pl.ds(0, n_dp - 1)]
    pltpu.make_async_copy(others_dp, others_dp, seq_recv).wait()
    partner_rows = jnp.zeros((seqs, LANES), jnp.float32)
    for j in range(seqs):
        row = all_seqs[pl.ds(ids[0, j] // seqs, 1), :]
        partner_rows = jnp.where(sub_s == j, row, partner_rows)
    partner_value = jnp.sum(
        jnp.where(lane_s == place_col, partner_rows, 0.0), axis=1, keepdims=True
    )
    margin_ref[...] = sign_col * (own_col - partner_value)
    pltpu.make_async_copy(others, others, row_send).wait()
    pltpu.make_async_copy(others_dp, others_dp, seq_send).wait()


def scale_kernel(grad_ref, margin_ref, out_hbm, loss_hbm, out_buf, loss_buf, sems):
    rows, width = out_buf.shape
    seqs = margin_ref.shape[0]
    length = rows // seqs
    margin = margin_ref[...]
    slope = -jax.nn.sigmoid(-margin)
    copies = []
    for j in range(seqs):
        here = pl.ds(j * length, length)
        out_buf[here, :] = grad_ref[here, :] * slope[j : j + 1, 0:1]
        copy = pltpu.make_async_copy(out_buf.at[here], out_hbm.at[here], sems.at[j])
        copy.start()
        copies.append(copy)
    loss = jnp.maximum(-margin, 0.0) + jnp.log1p(jnp.exp(-jnp.abs(margin)))
    sub = lax.broadcasted_iota(jnp.int32, (seqs, LANES), 0)
    lane = lax.broadcasted_iota(jnp.int32, (seqs, LANES), 1)
    loss_buf[...] = jnp.sum(jnp.where(sub == lane, loss, 0.0), axis=0)[:seqs]
    copy = pltpu.make_async_copy(loss_buf, loss_hbm, sems.at[seqs])
    copy.start()
    copies.append(copy)
    for copy in copies:
        copy.wait()


def shards(n_dp, n_tensor, n_z, *arrays):
    rows, width = arrays[0].shape
    seqs = arrays[4].shape[0]
    hbm = pl.BlockSpec(memory_space=pltpu.HBM)
    vmem = pl.BlockSpec(memory_space=pltpu.VMEM)
    arrays = [pltpu.with_memory_space_constraint(array, pltpu.HBM) for array in arrays]
    grad, margin = pl.pallas_call(
        functools.partial(stats_kernel, n_dp, n_tensor, n_z),
        out_shape=(
            pltpu.VMEM((rows, width), jnp.float32),
            pltpu.VMEM((seqs, LANES), jnp.float32),
        ),
        in_specs=[hbm] * 6,
        out_specs=(vmem, vmem),
        scratch_shapes=[
            pltpu.VMEM((rows, width), jnp.bfloat16),
            pltpu.VMEM((rows, width), jnp.bfloat16),
            pltpu.VMEM((2, rows), jnp.int32),
            pltpu.SMEM((2, seqs), jnp.int32),
            pltpu.VMEM((5, rows, LANES), jnp.float32),
            pltpu.VMEM((rows, LANES), jnp.int32),
            pltpu.VMEM((PARTS, LANES), jnp.float32),
            pltpu.VMEM((n_tensor, PARTS, LANES), jnp.float32),
            pltpu.VMEM((1, LANES), jnp.float32),
            pltpu.VMEM((n_dp, LANES), jnp.float32),
            pltpu.SemaphoreType.DMA((2, rows // GROUP)),
            pltpu.SemaphoreType.DMA((4,)),
            pltpu.SemaphoreType.DMA,
            pltpu.SemaphoreType.DMA,
            pltpu.SemaphoreType.DMA,
            pltpu.SemaphoreType.DMA,
            pltpu.SemaphoreType.REGULAR((3,)),
        ],
        compiler_params=pltpu.CompilerParams(
            collective_id=0, has_side_effects=True, vmem_limit_bytes=32 * 1024 * 1024
        ),
        name="row_stats",
    )(*arrays)
    return pl.pallas_call(
        scale_kernel,
        out_shape=(
            jax.ShapeDtypeStruct((rows, width), jnp.float32),
            jax.ShapeDtypeStruct((seqs,), jnp.float32),
        ),
        in_specs=[vmem, vmem],
        out_specs=(hbm, hbm),
        scratch_shapes=[
            pltpu.VMEM((rows, width), jnp.float32),
            pltpu.VMEM((seqs,), jnp.float32),
            pltpu.SemaphoreType.DMA((seqs + 1,)),
        ],
        compiler_params=pltpu.CompilerParams(vmem_limit_bytes=32 * 1024 * 1024),
        name="scale_grad",
    )(grad, margin)


def solution(mesh):
    n_dp, n_tensor = mesh.shape["dp"], mesh.shape["tensor"]
    n_z = 8 if n_dp % 8 == 0 and n_dp > 8 else n_dp // 2
    return jax.shard_map(
        functools.partial(shards, n_dp, n_tensor, n_z),
        mesh=mesh,
        in_specs=(P("dp", "tensor"), P("dp", "tensor"), P("dp"), P("dp"), P("dp"), P("dp")),
        out_specs=(P("dp", "tensor"), P("dp")),
        check_vma=False,
    )
```
